32 devices in a mesh: ctx: 4 (over y, x), dp: 8 (over z, core).
Axes of the slice: x: 2, y: 2, z: 4, core: 2. Of those that a mesh axis runs over, the one named last changes fastest.
Arguments:
- query_rows: bfloat16 [8, 512, 32, 128], P('dp', 'ctx'), may hold values from -6 to 6
- key_rows: bfloat16 [8, 512, 4, 128], P('dp', 'ctx'), may hold values from -6 to 6
- value_matrix: bfloat16 [8, 512, 4, 128], P('dp', 'ctx'), may hold values from -6 to 6
- out_grad: bfloat16 [8, 512, 32, 128], P('dp', 'ctx'), may hold values from -6 to 6
- offsets: int32 [8, 5], P('dp'), may hold values from 0 to 512, as said below
- query_head_group: int32 [32], replicated, may hold values from 0 to 3, as said below
Outputs:
- query_grad: bfloat16 [8, 512, 32, 128], P('dp', 'ctx')
- key_grad: bfloat16 [8, 512, 4, 128], P('dp', 'ctx')
The draws below stay inside these ranges and needn't reach their ends.
Inputs may be any that keep to these rules, and one draw needn't show every extreme that they name: offsets[b, 0] = 0 and offsets rise along each row; every pair holds 1 to 128 positions, and one pair of every sequence holds exactly 128; the positions from offsets[b, 4] to the end of the sequence are padding; the last sequence of the batch has no padding. `query_head_group`: each key and value head serves exactly 8 query heads.
All inputs are finite; a program needn't handle non-finite values.
Results may differ from the reference program's by a relative error of at most 0.005.
Values may be sent and summed in bfloat16 or wider, within the bound.
No kernel may reach another device: no remote copies, remote signals or barrier semaphores. Data moves between devices by JAX's collectives and lax.ppermute only.
A program may use at most 64 MiB of HBM per device.

```python
import math
import jax
import jax.numpy as jnp
from jax import lax

HQ = 32
KEY_VALUE_HEADS = 4
HEAD_SIZE = 128
TOKENS_PER_SHARD = 128
GROUP = 8
SEQUENCE_COUNT = 8
SEQUENCE_LENGTH = 512
PAIRS = 4
MOST = 128
TOKENS = 4096


def pair_offsets(key):
    base_key = jax.random.fold_in(key, 101)
    key_jitter = jax.random.fold_in(base_key, 1)
    key_length = jax.random.fold_in(base_key, 2)
    key_longest = jax.random.fold_in(base_key, 3)
    seq_index = jnp.arange(SEQUENCE_COUNT, dtype=jnp.int32)
    quarter = MOST // 4
    rising = quarter + 3 * quarter * seq_index // max(SEQUENCE_COUNT - 1, 1)
    jitter = jax.random.randint(key_jitter, (SEQUENCE_COUNT,), -(MOST // 8), MOST // 8 + 1)
    upper_len = jnp.clip(rising + jitter, max(quarter, 2), MOST)
    lower_len = jnp.maximum(upper_len // 2, 1)
    lengths = jax.random.randint(key_length, (SEQUENCE_COUNT, PAIRS), lower_len[:, None], upper_len[:, None] + 1)
    longest = jax.random.randint(key_longest, (SEQUENCE_COUNT,), 0, PAIRS)
    lengths = jnp.where(jnp.arange(PAIRS, dtype=jnp.int32)[None, :] == longest[:, None], MOST, lengths)
    lengths = jnp.where(seq_index[:, None] == SEQUENCE_COUNT - 1, MOST, lengths)
    bounds = jnp.cumsum(lengths, axis=1).astype(jnp.int32)
    return jnp.concatenate([jnp.zeros((SEQUENCE_COUNT, 1), jnp.int32), bounds], axis=1)


def draw_offsets(key, part):
    return pair_offsets(key)


def draw_query_head_group(key, part):
    shuffled = jax.random.permutation(jax.random.fold_in(key, 202), HQ)
    return (shuffled // GROUP).astype(jnp.int32)


def draw_query_rows(key, part):
    noise_key = jax.random.fold_in(key, 404)
    full_shape = (SEQUENCE_COUNT, SEQUENCE_LENGTH, HQ, HEAD_SIZE)
    drawn_rows = jnp.clip(jax.random.normal(noise_key, full_shape, jnp.float32), -4.0, 4.0)
    return drawn_rows.astype(jnp.bfloat16)


def draw_key_rows(key, part):
    noise_key = jax.random.fold_in(key, 505)
    full_shape = (SEQUENCE_COUNT, SEQUENCE_LENGTH, KEY_VALUE_HEADS, HEAD_SIZE)
    drawn_rows = jnp.clip(jax.random.normal(noise_key, full_shape, jnp.float32), -4.0, 4.0)
    return drawn_rows.astype(jnp.bfloat16)


def steps_of(rng, shape, split, least, high):
    def one(position, blocks):
        heights = jax.random.uniform(jax.random.fold_in(jax.random.fold_in(rng, 6), position), (blocks,), jnp.float32, least / len(split), high / len(split))
        return jnp.repeat(jnp.exp(heights), shape[position] // blocks).reshape((-1,) + (1,) * (len(shape) - position - 1))

    loudness = one(*split[0])
    for cut in split[1:]:
        loudness = loudness * one(*cut)
    return loudness


def gaussian(rng, dims, spread, limit, shards=(), kind=jnp.bfloat16):
    array = jax.random.normal(rng, dims, jnp.float32) * spread
    if len(shards) > 0:
        array = steps_of(rng, dims, shards, -0.22, 0.18) * array
    return jnp.clip(array, min=-limit, max=limit).astype(kind)


def setup_inputs(seed: int = 0) -> dict:
    keys = jax.random.split(jax.random.key(seed), 7)
    query_rows = draw_query_rows(jax.random.fold_in(keys[6], 71), 0)
    key_rows = draw_key_rows(jax.random.fold_in(keys[6], 71), 0)
    value_matrix = gaussian(keys[2], (SEQUENCE_COUNT, SEQUENCE_LENGTH, KEY_VALUE_HEADS, HEAD_SIZE), 1.0, 6.0, ((0, 8), (1, 4)))
    out_grad = gaussian(keys[3], (SEQUENCE_COUNT, SEQUENCE_LENGTH, HQ, HEAD_SIZE), 1.0, 6.0, ((0, 8), (1, 4)))
    offsets = draw_offsets(jax.random.fold_in(keys[6], 71), 0)
    query_head_group = draw_query_head_group(jax.random.fold_in(keys[6], 71), 0)
    return {"query_rows": query_rows, "key_rows": key_rows, "value_matrix": value_matrix, "out_grad": out_grad, "offsets": offsets, "query_head_group": query_head_group}


def pair_index(bounds, positions):
    inner_bounds = bounds[1:]
    found_count = lax.optimization_barrier(jnp.sum((positions[:, None] >= inner_bounds[None, :]).astype(jnp.int32), axis=1))
    return jnp.where(positions < 0, -1, found_count).astype(jnp.int32)

def sequence_grads(seq_items, query_head_group, grad_scale):
    query_seq, key_seq, value_seq, grad_seq, bounds = seq_items
    block_rows = min(512, SEQUENCE_LENGTH)
    window = block_rows + TOKENS_PER_SHARD
    inv_root = 1.0 / math.sqrt(HEAD_SIZE)
    padded_rows = jnp.zeros((TOKENS_PER_SHARD, KEY_VALUE_HEADS, HEAD_SIZE), jnp.float32)
    key_pad = jnp.concatenate([padded_rows, key_seq.astype(jnp.float32)], axis=0)
    value_pad = jnp.concatenate([padded_rows, value_seq.astype(jnp.float32)], axis=0)
    group_member = (query_head_group[:, None] == jnp.arange(KEY_VALUE_HEADS, dtype=jnp.int32)[None, :]).astype(jnp.float32)

    def block_step(key_acc, block_number):
        row_start = block_number * block_rows
        rows_query = lax.dynamic_slice_in_dim(query_seq, row_start, block_rows, 0).astype(jnp.float32)
        rows_grad = lax.dynamic_slice_in_dim(grad_seq, row_start, block_rows, 0).astype(jnp.float32)
        keys_win = lax.dynamic_slice_in_dim(key_pad, row_start, window, 0)[:, query_head_group, :]
        values_win = lax.dynamic_slice_in_dim(value_pad, row_start, window, 0)[:, query_head_group, :]
        pos_rows = row_start + jnp.arange(block_rows, dtype=jnp.int32)
        pos_cols = row_start - TOKENS_PER_SHARD + jnp.arange(window, dtype=jnp.int32)
        pair_rows = pair_index(bounds, pos_rows)
        pair_cols = pair_index(bounds, pos_cols)
        visible = (pair_rows[:, None] == pair_cols[None, :]) & (pair_rows[:, None] < PAIRS) & (pos_cols[None, :] <= pos_rows[:, None])
        scores = jnp.einsum('rhd,khd->hrk', rows_query, keys_win) * inv_root
        row_live = jnp.any(visible, axis=1)
        row_top = lax.optimization_barrier(jnp.max(jnp.where(visible, scores, -1e+30), axis=-1, keepdims=True))
        row_top = jnp.where(row_live[:, None], row_top, 0.0)
        expo_terms = jnp.where(visible, jnp.exp(scores - row_top), 0.0)
        totals = lax.optimization_barrier(jnp.sum(expo_terms, axis=-1, keepdims=True)) + jnp.where(row_live, 0.0, 1.0)[:, None]
        attn_prob = expo_terms / totals
        prob_grad = jnp.einsum('rhd,khd->hrk', rows_grad, values_win)
        row_delta = lax.optimization_barrier(jnp.sum(attn_prob * prob_grad, axis=-1, keepdims=True))
        score_grad = lax.optimization_barrier((attn_prob * (prob_grad - row_delta)).astype(jnp.bfloat16)).astype(jnp.float32)
        grad_rows = jnp.einsum('hrk,khd->rhd', score_grad, keys_win)
        key_heads = jnp.einsum('hrk,rhd->khd', score_grad, rows_query)
        key_part = jnp.einsum('khd,hg->kgd', key_heads, group_member)
        key_acc = lax.dynamic_update_slice_in_dim(key_acc, lax.dynamic_slice_in_dim(key_acc, row_start, window, 0) + key_part, row_start, 0)
        return (key_acc, grad_rows)
    empty_accumulator = jnp.zeros((SEQUENCE_LENGTH + TOKENS_PER_SHARD, KEY_VALUE_HEADS, HEAD_SIZE), jnp.float32)
    key_acc, grad_blocks = lax.scan(block_step, empty_accumulator, jnp.arange(SEQUENCE_LENGTH // block_rows, dtype=jnp.int32))
    q_factor = grad_scale * inv_root
    query_grad = (grad_blocks.reshape(SEQUENCE_LENGTH, HQ, HEAD_SIZE) * q_factor).astype(jnp.bfloat16)
    key_grad = (key_acc[TOKENS_PER_SHARD:] * q_factor).astype(jnp.bfloat16)
    return (query_grad, key_grad)

def reference(query_rows, key_rows, value_matrix, out_grad, offsets, query_head_group):
    count = jnp.sum(offsets[:, PAIRS])
    grad_scale = jnp.float32(TOKENS) / count.astype(jnp.float32)

    def one_sequence(seq_items):
        return sequence_grads(seq_items, query_head_group, grad_scale)
    query_grad, key_grad = lax.map(one_sequence, (query_rows, key_rows, value_matrix, out_grad, offsets))
    return (query_grad, key_grad)
```

```python
import functools
import math

import jax
import jax.numpy as jnp
from jax import lax
from jax.experimental import pallas as pl
from jax.experimental.pallas import tpu as pltpu
from jax.sharding import PartitionSpec as P

NT = (((1,), (1,)), ((), ()))
NN = (((1,), (0,)), ((), ()))
F32, BF16 = jnp.float32, jnp.bfloat16
BLOCK = 256
CHUNK = 128


def dot(a, b, dims=NN):
    return lax.dot_general(a, b, dims, preferred_element_type=F32)


def split_heads(packed, flat, out, rows, groups, first):
    flat[...] = packed[...].astype(F32)
    for g in range(groups):
        out[g, first : first + rows, :] = flat[pl.ds(g, rows, stride=groups), :].astype(BF16)


def arrange_kernel(sizes, bounds, group, query, grad, key, value, sorted_query, sorted_grad, query_t, unsort, bias, own_key, own_value, flat):
    tok, heads, groups, per = sizes
    step = BLOCK // heads
    share = step * per
    lanes = lax.broadcasted_iota(jnp.int32, (8, BLOCK), 1)
    head = lanes % heads
    seen = [jnp.int32(0)] * groups
    target = (lanes // heads) * per
    for h in range(heads):
        mine = group[h]
        slot = mine * share
        for g in range(groups):
            here = mine == g
            slot = slot + jnp.where(here, seen[g], 0)
            seen[g] = seen[g] + jnp.where(here, 1, 0)
        target = target + jnp.where(head == h, slot, 0)
    rows = lax.broadcasted_iota(jnp.int32, (BLOCK, BLOCK), 0)
    sort = jnp.where(rows == target[:1], 1.0, 0.0).astype(F32)
    unsort[...] = sort.T.astype(BF16)
    sort = sort.astype(BF16)
    for b in range(tok // step):
        part = slice(b * BLOCK, (b + 1) * BLOCK)
        both = jnp.concatenate([query[part, :], grad[part, :]], axis=1)
        both = dot(sort, both).astype(BF16)
        depth = query.shape[1]
        for g in range(groups):
            sorted_query[g, b * share : (b + 1) * share, :] = both[g * share : (g + 1) * share, :depth]
            sorted_grad[g, b * share : (b + 1) * share, :] = both[g * share : (g + 1) * share, depth:]
    for g in range(groups):
        query_t[g] = sorted_query[g].T
    split_heads(key, flat, own_key, tok, groups, 0)
    split_heads(value, flat, own_value, tok, groups, 0)
    start = lax.axis_index("ctx") * tok
    cube = (tok, per, tok)
    row = lax.broadcasted_iota(jnp.int32, cube, 0).reshape(tok * per, tok)
    col = lax.broadcasted_iota(jnp.int32, (tok * per, tok), 1)
    place = row + start
    low = jnp.zeros_like(place)
    last = bounds.shape[1] - 1
    for i in range(1, last):
        low = jnp.where(place >= bounds[0, i], bounds[0, i], low)
    low = jnp.where(place >= bounds[0, last], jnp.int32(1 << 30), low)
    where = start + col - jnp.where(col > row, tok, 0)
    bias[...] = jnp.where(where >= low, 0.0, -1e30).astype(F32)


def score_kernel(sizes, bias, query, grad, query_t, own_key, own_value, back_key, back_value, score_grad, keys, own_t, back, values, flat):
    tok, heads, groups, per = sizes
    depth = query.shape[2]
    split_heads(back_key, flat, keys, tok, groups, tok)
    split_heads(back_value, flat, values, tok, groups, tok)
    keys[:, :tok, :] = own_key[...]
    values[:, :tok, :] = own_value[...]
    rate = math.log2(math.e) / math.sqrt(depth)

    def one_group(g, carry):
        for c in range(tok * per // CHUNK):
            part = slice(c * CHUNK, (c + 1) * CHUNK)
            here = CHUNK // per
            row = c * here + lax.broadcasted_iota(jnp.int32, (here, per, tok), 0).reshape(CHUNK, tok)
            own = lax.broadcasted_iota(jnp.int32, (CHUNK, tok), 1) <= row
            two = dot(query[g, part, :], keys[g], NT)
            scores = jnp.where(own, two[:, :tok], two[:, tok:]) + bias[part, :]
            two = dot(grad[g, part, :], values[g], NT)
            prob_grad = jnp.where(own, two[:, :tok], two[:, tok:])
            top = jnp.maximum(jnp.max(scores, axis=1, keepdims=True), -1e29)
            terms = jnp.exp2((scores - top) * rate)
            scale = 1.0 / jnp.maximum(jnp.sum(terms, axis=1, keepdims=True), 1.0)
            delta = jnp.sum(terms * prob_grad, axis=1, keepdims=True) * scale
            out = (terms * scale) * (prob_grad - delta)
            score_grad[g, part, :tok] = jnp.where(own, out, 0.0).astype(BF16)
            score_grad[g, part, tok:] = jnp.where(own, 0.0, out).astype(BF16)
        both = dot(query_t[g], score_grad[g])
        own_t[g] = both[:, :tok]
        flat[pl.ds(g, tok, stride=groups), :] = both[:, tok:].T
        return carry

    lax.fori_loop(0, groups, one_group, 0)
    back[...] = flat[...].astype(BF16)


def factor_of(count, tokens, depth):
    last = count.shape[1] - 1
    return (tokens / count[0:1, last : last + 1].astype(F32)) * (1.0 / math.sqrt(depth))


def query_kernel(sizes, tokens, count, score_grad, keys, unsort, own_t, query_grad, key_grad, part_grad):
    tok, heads, groups, per = sizes
    depth = keys.shape[2]
    factor = factor_of(count, tokens, depth)
    step = BLOCK // heads
    share = step * per

    def one_group(g, carry):
        for c in range(tok * per // BLOCK):
            part = slice(c * BLOCK, (c + 1) * BLOCK)
            part_grad[g, part, :] = (dot(score_grad[g, part, :], keys[g]) * factor).astype(BF16)
        key_grad[pl.ds(g, tok, stride=groups), :] = own_t[g].T
        return carry

    lax.fori_loop(0, groups, one_group, 0)
    for b in range(0, tok // step, 2):
        both = [
            jnp.concatenate([part_grad[g, (b + i) * share : (b + i + 1) * share, :] for g in range(groups)], axis=0)
            for i in range(2)
        ]
        both = dot(unsort[...], jnp.concatenate(both, axis=1)).astype(BF16)
        query_grad[b * BLOCK : (b + 1) * BLOCK, :] = both[:, :depth]
        query_grad[(b + 1) * BLOCK : (b + 2) * BLOCK, :] = both[:, depth:]


def key_kernel(tokens, count, own, back, key_grad):
    factor = factor_of(count, tokens, own.shape[1])
    key_grad[...] = ((own[...] + back[...].astype(F32)) * factor).astype(BF16)


VMEM = pl.BlockSpec(memory_space=pltpu.VMEM)
SMEM = pl.BlockSpec(memory_space=pltpu.SMEM)


def call(kernel, ins, outs, scratch=()):
    return pl.pallas_call(
        kernel,
        out_shape=[jax.ShapeDtypeStruct(shape, dtype) for shape, dtype in outs],
        in_specs=ins,
        out_specs=[VMEM] * len(outs),
        scratch_shapes=[pltpu.VMEM(shape, dtype) for shape, dtype in scratch],
        compiler_params=pltpu.CompilerParams(vmem_limit_bytes=32 * 1024 * 1024),
    )


def sum_over(value, axis):
    size = lax.axis_size(axis)
    if size & (size - 1):
        return lax.psum(value, axis)
    hop = 1
    while hop < size:
        value = value + lax.ppermute(value, axis, [(i, i ^ hop) for i in range(size)])
        hop *= 2
    return value


def per_device(query_rows, key_rows, value_matrix, out_grad, offsets, query_head_group):
    _, tok, heads, depth = query_rows.shape
    groups = key_rows.shape[2]
    per = heads // groups
    sizes = (tok, heads, groups, per)
    ctx = lax.axis_size("ctx")
    tokens = float(offsets.shape[0] * lax.axis_size("dp") * tok * ctx)
    ahead = [(i, (i + 1) % ctx) for i in range(ctx)]
    behind = [((i + 1) % ctx, i) for i in range(ctx)]

    back_key = lax.ppermute(key_rows, "ctx", ahead).reshape(tok * groups, depth)
    back_value = lax.ppermute(value_matrix, "ctx", ahead).reshape(tok * groups, depth)
    count = sum_over(offsets, "dp")

    sorted_shape = (groups, tok * per, depth)
    sorted_query, sorted_grad, query_t, unsort, bias, own_key, own_value = call(
        functools.partial(arrange_kernel, sizes),
        [SMEM, SMEM, VMEM, VMEM, VMEM, VMEM],
        [
            (sorted_shape, BF16),
            (sorted_shape, BF16),
            ((groups, depth, tok * per), BF16),
            ((BLOCK, BLOCK), BF16),
            ((tok * per, tok), F32),
            ((groups, tok, depth), BF16),
            ((groups, tok, depth), BF16),
        ],
        [((tok * groups, depth), F32)],
    )(
        offsets,
        query_head_group,
        query_rows.reshape(tok * heads, depth),
        out_grad.reshape(tok * heads, depth),
        key_rows.reshape(tok * groups, depth),
        value_matrix.reshape(tok * groups, depth),
    )

    score_grad, keys, own_t, back = call(
        functools.partial(score_kernel, sizes),
        [VMEM] * 8,
        [
            ((groups, tok * per, 2 * tok), BF16),
            ((groups, 2 * tok, depth), BF16),
            ((groups, depth, tok), F32),
            ((tok * groups, depth), BF16),
        ],
        [((groups, 2 * tok, depth), BF16), ((tok * groups, depth), F32)],
    )(bias, sorted_query, sorted_grad, query_t, own_key, own_value, back_key, back_value)

    back = lax.ppermute(back, "ctx", behind)

    query_grad, own = call(
        functools.partial(query_kernel, sizes, tokens),
        [VMEM] * 5,
        [((tok * heads, depth), BF16), ((tok * groups, depth), F32)],
        [(sorted_shape, BF16)],
    )(count, score_grad, keys, unsort, own_t)
    (key_grad,) = call(
        functools.partial(key_kernel, tokens), [VMEM] * 3, [((tok * groups, depth), BF16)]
    )(count, own, back)
    return (query_grad.reshape(query_rows.shape), key_grad.reshape(key_rows.shape))


def solution(mesh):
    return jax.shard_map(
        per_device,
        mesh=mesh,
        in_specs=(
            P("dp", "ctx", None, None),
            P("dp", "ctx", None, None),
            P("dp", "ctx", None, None),
            P("dp", "ctx", None, None),
            P("dp", None),
            P(),
        ),
        out_specs=(P("dp", "ctx", None, None), P("dp", "ctx", None, None)),
        check_vma=False,
    )
```

```python
import functools
import math

import jax
import jax.numpy as jnp
from jax import lax
from jax.experimental import pallas as pl
from jax.experimental.pallas import tpu as pltpu
from jax.sharding import PartitionSpec as P

NT = (((1,), (1,)), ((), ()))
NN = (((1,), (0,)), ((), ()))
TN = (((0,), (0,)), ((), ()))
F32, BF16 = jnp.float32, jnp.bfloat16
BLOCK = 256


def dot(a, b, dims=NN):
    return lax.dot_general(a, b, dims, preferred_element_type=F32)


def stack(*spans):
    pieces = [v[a:b] for v, a, b in spans if b > a]
    return pieces[0] if len(pieces) == 1 else jnp.concatenate(pieces, axis=0)


def split_heads(packed, flat, out, rows, groups):
    flat[...] = packed[...].astype(F32)
    for g in range(groups):
        out[g] = flat[pl.ds(g, rows, stride=groups), :].astype(BF16)


def arrange_kernel(sizes, bounds_in, group_in, query_in, grad_in, key_in, value_in, sorted_query, sorted_grad, unsort, bias, own_key, own_value, bounds, group, query, grad, key, value, flat, sems):
    tok, heads, groups, per = sizes
    step = BLOCK // heads
    share = step * per
    depth = query.shape[1]
    copies = [
        pltpu.make_async_copy(a, b, sems.at[i])
        for i, (a, b) in enumerate(
            [(group_in, group), (bounds_in, bounds), (query_in, query), (grad_in, grad), (key_in, key), (value_in, value)]
        )
    ]
    for copy in copies:
        copy.start()
    copies[0].wait()
    lanes = lax.broadcasted_iota(jnp.int32, (8, BLOCK), 1)
    head = lanes % heads
    seen = [jnp.int32(0)] * groups
    target = (lanes // heads) * per
    for h in range(heads):
        mine = group[h]
        slot = mine * share
        for g in range(groups):
            here = mine == g
            slot = slot + jnp.where(here, seen[g], 0)
            seen[g] = seen[g] + jnp.where(here, 1, 0)
        target = target + jnp.where(head == h, slot, 0)
    rows = lax.broadcasted_iota(jnp.int32, (BLOCK, BLOCK), 0)
    sort = jnp.where(rows == target[:1], 1.0, 0.0).astype(F32)
    unsort[...] = sort.T.astype(BF16)
    sort = sort.astype(BF16)
    copies[1].wait()
    start = lax.axis_index("ctx") * tok
    row = lax.broadcasted_iota(jnp.int32, (8, tok * per), 1) // per
    place = row + start
    low = jnp.zeros_like(place)
    last = bounds.shape[1] - 1
    for i in range(1, last):
        low = jnp.where(place >= bounds[0, i], bounds[0, i], low)
    low = jnp.where(place >= bounds[0, last], jnp.int32(1 << 30), low) - start
    for c in range(0, tok, 8):
        col = c + lax.broadcasted_iota(jnp.int32, (8, tok * per), 0)
        where = col - jnp.where(col > row, tok, 0)
        bias[c : c + 8, :] = jnp.where(where >= low, 0.0, -1e30).astype(F32)
    for copy in copies[2:]:
        copy.wait()
    for b in range(tok // step):
        part = slice(b * BLOCK, (b + 1) * BLOCK)
        both = jnp.concatenate([query[part, :], grad[part, :]], axis=1)
        both = dot(sort, both).astype(BF16)
        for g in range(groups):
            sorted_query[g, b * share : (b + 1) * share, :] = both[g * share : (g + 1) * share, :depth]
            sorted_grad[g, b * share : (b + 1) * share, :] = both[g * share : (g + 1) * share, depth:]
    split_heads(key, flat, own_key, tok, groups)
    split_heads(value, flat, own_value, tok, groups)


def score_kernel(sizes, bias, query, grad, own_key, own_value, back_in, value_in, score_grad, back_key, own_grad, back, back_value, flat):
    tok, heads, groups, per = sizes
    depth = query.shape[2]
    split_heads(back_in, flat, back_key, tok, groups)
    split_heads(value_in, flat, back_value, tok, groups)
    rate = math.log2(math.e) / math.sqrt(depth)
    here = BLOCK // per
    own = lax.broadcasted_iota(jnp.int32, (here, BLOCK), 0) <= lax.broadcasted_iota(jnp.int32, (here, BLOCK), 1) // per
    for g in range(groups):
        for t in range(tok // here):
            part = slice(t * BLOCK, (t + 1) * BLOCK)
            lo, hi = t * here, (t + 1) * here

            def product(left, right, rows):
                a, b = dot(left[g, :hi], rows, NT), dot(right[g, lo:], rows, NT)
                return stack((a, 0, lo), (jnp.where(own, a[lo:], b[:here]), 0, here), (b, here, tok - lo))

            scores = product(own_key, back_key, query[g, part, :]) + bias[:, part]
            prob_grad = product(own_value, back_value, grad[g, part, :])
            top = jnp.maximum(jnp.max(scores, axis=0, keepdims=True), -1e29)
            terms = jnp.exp2((scores - top) * rate)
            scale = 1.0 / jnp.maximum(jnp.sum(terms, axis=0, keepdims=True), 1.0)
            delta = jnp.sum(terms * prob_grad, axis=0, keepdims=True) * scale
            out = (terms * scale) * (prob_grad - delta)
            mid = out[lo:hi]
            score_grad[g, t, :hi, :] = stack((out, 0, lo), (jnp.where(own, mid, 0.0), 0, here)).astype(BF16)
            score_grad[g, t, hi:, :] = stack((jnp.where(own, 0.0, mid), 0, here), (out, hi, tok)).astype(BF16)
    for g in range(groups):
        own_sum, back_sum = [None] * (tok // here), [None] * (tok // here)
        for t in range(tok // here):
            both = dot(score_grad[g, t], query[g, t * BLOCK : (t + 1) * BLOCK, :])
            for i in range(t + 1):
                piece = both[i * here : (i + 1) * here]
                own_sum[i] = piece if own_sum[i] is None else own_sum[i] + piece
            for i in range(t, tok // here):
                piece = both[(i + 1) * here : (i + 2) * here]
                back_sum[i] = piece if back_sum[i] is None else back_sum[i] + piece
        own_grad[g] = jnp.concatenate(own_sum, axis=0)
        flat[pl.ds(g, tok, stride=groups), :] = jnp.concatenate(back_sum, axis=0)
    back[...] = flat[...].astype(BF16)


def factor_of(count, tokens, depth):
    last = count.shape[1] - 1
    return (tokens / count[0:1, last : last + 1].astype(F32)) * (1.0 / math.sqrt(depth))


def query_kernel(sizes, score_grad, own_key, back_key, own_grad, part_grad, key_grad):
    tok, heads, groups, per = sizes
    here = BLOCK // per
    for g in range(groups):
        for t in range(tok // here):
            keys = jnp.concatenate([own_key[g, : (t + 1) * here], back_key[g, t * here :]], axis=0)
            part_grad[g, t * BLOCK : (t + 1) * BLOCK, :] = dot(score_grad[g, t], keys, TN)
        key_grad[pl.ds(g, tok, stride=groups), :] = own_grad[g]


def unsort_kernel(sizes, tokens, count, part_grad, unsort, query_grad):
    tok, heads, groups, per = sizes
    depth = part_grad.shape[2]
    factor = factor_of(count, tokens, depth)
    step = BLOCK // heads
    share = step * per
    for b in range(0, tok // step, 2):
        both = [
            jnp.concatenate([part_grad[g, (b + i) * share : (b + i + 1) * share, :] for g in range(groups)], axis=0)
            for i in range(2)
        ]
        both = (jnp.concatenate(both, axis=1) * factor).astype(BF16)
        both = dot(unsort[...], both).astype(BF16)
        query_grad[b * BLOCK : (b + 1) * BLOCK, :] = both[:, :depth]
        query_grad[(b + 1) * BLOCK : (b + 2) * BLOCK, :] = both[:, depth:]


def key_kernel(tokens, count, own, back, key_grad):
    factor = factor_of(count, tokens, own.shape[1])
    key_grad[...] = ((own[...] + back[...].astype(F32)) * factor).astype(BF16)


VMEM = pl.BlockSpec(memory_space=pltpu.VMEM)
HBM = pl.BlockSpec(memory_space=pltpu.HBM)


def call(kernel, ins, outs, scratch=()):
    return pl.pallas_call(
        kernel,
        out_shape=[jax.ShapeDtypeStruct(shape, dtype) for shape, dtype in outs],
        in_specs=ins,
        out_specs=[VMEM] * len(outs),
        scratch_shapes=list(scratch),
        compiler_params=pltpu.CompilerParams(vmem_limit_bytes=32 * 1024 * 1024),
    )


def add_partner(value, axis, hop):
    return value + lax.ppermute(value, axis, [(i, i ^ hop) for i in range(lax.axis_size(axis))])


def per_device(query_rows, key_rows, value_matrix, out_grad, offsets, query_head_group):
    _, tok, heads, depth = query_rows.shape
    groups = key_rows.shape[2]
    per = heads // groups
    sizes = (tok, heads, groups, per)
    ctx = lax.axis_size("ctx")
    tokens = float(offsets.shape[0] * lax.axis_size("dp") * tok * ctx)
    ahead = [(i, (i + 1) % ctx) for i in range(ctx)]
    behind = [((i + 1) % ctx, i) for i in range(ctx)]

    back_key = lax.ppermute(key_rows, "ctx", ahead).reshape(tok * groups, depth)
    back_value = lax.ppermute(value_matrix, "ctx", ahead).reshape(tok * groups, depth)
    dp = lax.axis_size("dp")
    paired = dp >= 4 and dp & (dp - 1) == 0
    hops = [1 << i for i in range(dp.bit_length() - 1)] if paired else []
    count = add_partner(offsets, "dp", 1) if paired else lax.psum(offsets, "dp")

    sorted_shape = (groups, tok * per, depth)
    packed = (tok * groups, depth)
    split = (groups, tok, depth)
    here = BLOCK // per
    sorted_query, sorted_grad, unsort, bias, own_key, own_value = call(
        functools.partial(arrange_kernel, sizes),
        [HBM] * 6,
        [
            (sorted_shape, BF16),
            (sorted_shape, BF16),
            ((BLOCK, BLOCK), BF16),
            ((tok, tok * per), F32),
            (split, BF16),
            (split, BF16),
        ],
        [
            pltpu.SMEM(offsets.shape, jnp.int32),
            pltpu.SMEM((heads,), jnp.int32),
            pltpu.VMEM((tok * heads, depth), BF16),
            pltpu.VMEM((tok * heads, depth), BF16),
            pltpu.VMEM(packed, BF16),
            pltpu.VMEM(packed, BF16),
            pltpu.VMEM(packed, F32),
            pltpu.SemaphoreType.DMA((6,)),
        ],
    )(
        *[
            pltpu.with_memory_space_constraint(x, pltpu.HBM)
            for x in (
                offsets,
                query_head_group,
                query_rows.reshape(tok * heads, depth),
                out_grad.reshape(tok * heads, depth),
                key_rows.reshape(packed),
                value_matrix.reshape(packed),
            )
        ]
    )

    count, unsort = lax.optimization_barrier((count, unsort))
    for hop in hops[1:-1]:
        count = add_partner(count, "dp", hop)

    score_grad, back_key, own, back = call(
        functools.partial(score_kernel, sizes),
        [VMEM] * 7,
        [
            ((groups, tok // here, tok + here, BLOCK), BF16),
            (split, BF16),
            (split, F32),
            (packed, BF16),
        ],
        [pltpu.VMEM(split, BF16), pltpu.VMEM(packed, F32)],
    )(bias, sorted_query, sorted_grad, own_key, own_value, back_key, back_value)

    count, back = lax.optimization_barrier((count, back))
    back = lax.ppermute(back, "ctx", behind)
    for hop in hops[-1:]:
        count = add_partner(count, "dp", hop)

    part_grad, own = call(
        functools.partial(query_kernel, sizes), [VMEM] * 4, [(sorted_shape, F32), (packed, F32)]
    )(score_grad, own_key, back_key, own)
    (query_grad,) = call(
        functools.partial(unsort_kernel, sizes, tokens), [VMEM] * 3, [((tok * heads, depth), BF16)]
    )(count, part_grad, unsort)
    (key_grad,) = call(
        functools.partial(key_kernel, tokens), [VMEM] * 3, [((tok * groups, depth), BF16)]
    )(count, own, back)
    return (query_grad.reshape(query_rows.shape), key_grad.reshape(key_rows.shape))


def solution(mesh):
    return jax.shard_map(
        per_device,
        mesh=mesh,
        in_specs=(
            P("dp", "ctx", None, None),
            P("dp", "ctx", None, None),
            P("dp", "ctx", None, None),
            P("dp", "ctx", None, None),
            P("dp", None),
            P(),
        ),
        out_specs=(P("dp", "ctx", None, None), P("dp", "ctx", None, None)),
        check_vma=False,
    )
```

```python
import functools
import math

import jax
import jax.numpy as jnp
from jax import lax
from jax.experimental import pallas as pl
from jax.experimental.pallas import tpu as pltpu
from jax.sharding import PartitionSpec as P

NT = (((1,), (1,)), ((), ()))
NN = (((1,), (0,)), ((), ()))
TN = (((0,), (0,)), ((), ()))
F32, BF16 = jnp.float32, jnp.bfloat16
BLOCK = 256


def dot(a, b, dims=NN):
    return lax.dot_general(a, b, dims, preferred_element_type=F32)


def stack(*spans):
    pieces = [v[a:b] for v, a, b in spans if b > a]
    return pieces[0] if len(pieces) == 1 else jnp.concatenate(pieces, axis=0)


def split_heads(packed, flat, out, rows, groups):
    flat[...] = packed[...].astype(F32)
    for g in range(groups):
        out[g] = flat[pl.ds(g, rows, stride=groups), :].astype(BF16)


def arrange_kernel(sizes, bounds_in, group_in, query_in, grad_in, key_in, value_in, sorted_query, sorted_grad, unsort, bias, own_key, own_value, bounds, group, query, grad, key, value, flat, sems):
    tok, heads, groups, per = sizes
    step = BLOCK // heads
    share = step * per
    depth = query.shape[1]
    copies = [
        pltpu.make_async_copy(a, b, sems.at[i])
        for i, (a, b) in enumerate(
            [(group_in, group), (bounds_in, bounds), (query_in, query), (grad_in, grad), (key_in, key), (value_in, value)]
        )
    ]
    for copy in copies:
        copy.start()
    copies[0].wait()
    lanes = lax.broadcasted_iota(jnp.int32, (8, BLOCK), 1)
    head = lanes % heads
    seen = [jnp.int32(0)] * groups
    target = (lanes // heads) * per
    for h in range(heads):
        mine = group[h]
        slot = mine * share
        for g in range(groups):
            here = mine == g
            slot = slot + jnp.where(here, seen[g], 0)
            seen[g] = seen[g] + jnp.where(here, 1, 0)
        target = target + jnp.where(head == h, slot, 0)
    rows = lax.broadcasted_iota(jnp.int32, (BLOCK, BLOCK), 0)
    sort = jnp.where(rows == target[:1], 1.0, 0.0).astype(F32)
    unsort[...] = sort.T.astype(BF16)
    sort = sort.astype(BF16)
    copies[1].wait()
    start = lax.axis_index("ctx") * tok
    row = lax.broadcasted_iota(jnp.int32, (8, tok * per), 1) // per
    place = row + start
    low = jnp.zeros_like(place)
    last = bounds.shape[1] - 1
    for i in range(1, last):
        low = jnp.where(place >= bounds[0, i], bounds[0, i], low)
    low = jnp.where(place >= bounds[0, last], jnp.int32(1 << 30), low) - start
    for c in range(0, tok, 8):
        col = c + lax.broadcasted_iota(jnp.int32, (8, tok * per), 0)
        where = col - jnp.where(col > row, tok, 0)
        bias[c : c + 8, :] = jnp.where(where >= low, 0.0, -1e30).astype(F32)
    for copy in copies[2:]:
        copy.wait()
    for b in range(tok // step):
        part = slice(b * BLOCK, (b + 1) * BLOCK)
        both = jnp.concatenate([query[part, :], grad[part, :]], axis=1)
        both = dot(sort, both).astype(BF16)
        for g in range(groups):
            sorted_query[g, b * share : (b + 1) * share, :] = both[g * share : (g + 1) * share, :depth]
            sorted_grad[g, b * share : (b + 1) * share, :] = both[g * share : (g + 1) * share, depth:]
    split_heads(key, flat, own_key, tok, groups)
    split_heads(value, flat, own_value, tok, groups)


def own_mask(per):
    here = BLOCK // per
    shape = (here, BLOCK)
    return lax.broadcasted_iota(jnp.int32, shape, 0) <= lax.broadcasted_iota(jnp.int32, shape, 1) // per


def product(left, right, g, t, rows, own):
    here, tok = own.shape[0], left.shape[1]
    lo, hi = t * here, (t + 1) * here
    a, b = dot(left[g, :hi], rows, NT), dot(right[g, lo:], rows, NT)
    return stack((a, 0, lo), (jnp.where(own, a[lo:], b[:here]), 0, here), (b, here, tok - lo))


def probs_kernel(sizes, bias, query, own_key, back_in, probs, back_key, flat):
    tok, heads, groups, per = sizes
    split_heads(back_in, flat, back_key, tok, groups)
    rate = math.log2(math.e) / math.sqrt(query.shape[2])
    own = own_mask(per)
    for g in range(groups):
        for t in range(tok * per // BLOCK):
            part = slice(t * BLOCK, (t + 1) * BLOCK)
            scores = product(own_key, back_key, g, t, query[g, part, :], own) + bias[:, part]
            top = jnp.maximum(jnp.max(scores, axis=0, keepdims=True), -1e29)
            terms = jnp.exp2((scores - top) * rate)
            scale = 1.0 / jnp.maximum(jnp.sum(terms, axis=0, keepdims=True), 1.0)
            probs[g, :, part] = terms * scale


def score_kernel(sizes, probs, query, grad, own_value, value_in, score_grad, own_grad, back, back_value, flat):
    tok, heads, groups, per = sizes
    split_heads(value_in, flat, back_value, tok, groups)
    here = BLOCK // per
    own = own_mask(per)
    for g in range(groups):
        for t in range(tok // here):
            part = slice(t * BLOCK, (t + 1) * BLOCK)
            lo, hi = t * here, (t + 1) * here
            prob = probs[g, :, part]
            prob_grad = product(own_value, back_value, g, t, grad[g, part, :], own)
            delta = jnp.sum(prob * prob_grad, axis=0, keepdims=True)
            out = prob * (prob_grad - delta)
            mid = out[lo:hi]
            score_grad[g, t, :hi, :] = stack((out, 0, lo), (jnp.where(own, mid, 0.0), 0, here)).astype(BF16)
            score_grad[g, t, hi:, :] = stack((jnp.where(own, 0.0, mid), 0, here), (out, hi, tok)).astype(BF16)
    for g in range(groups):
        own_sum, back_sum = [None] * (tok // here), [None] * (tok // here)
        for t in range(tok // here):
            both = dot(score_grad[g, t], query[g, t * BLOCK : (t + 1) * BLOCK, :])
            for i in range(t + 1):
                piece = both[i * here : (i + 1) * here]
                own_sum[i] = piece if own_sum[i] is None else own_sum[i] + piece
            for i in range(t, tok // here):
                piece = both[(i + 1) * here : (i + 2) * here]
                back_sum[i] = piece if back_sum[i] is None else back_sum[i] + piece
        own_grad[g] = jnp.concatenate(own_sum, axis=0)
        flat[pl.ds(g, tok, stride=groups), :] = jnp.concatenate(back_sum, axis=0)
    back[...] = flat[...].astype(BF16)


def factor_of(count, tokens, depth):
    last = count.shape[1] - 1
    return (tokens / count[0:1, last : last + 1].astype(F32)) * (1.0 / math.sqrt(depth))


def query_kernel(sizes, score_grad, own_key, back_key, own_grad, part_grad, key_grad):
    tok, heads, groups, per = sizes
    here = BLOCK // per
    for g in range(groups):
        for t in range(tok // here):
            keys = jnp.concatenate([own_key[g, : (t + 1) * here], back_key[g, t * here :]], axis=0)
            part_grad[g, t * BLOCK : (t + 1) * BLOCK, :] = dot(score_grad[g, t], keys, TN)
        key_grad[pl.ds(g, tok, stride=groups), :] = own_grad[g]


def unsort_kernel(sizes, tokens, count, part_grad, unsort, query_grad):
    tok, heads, groups, per = sizes
    depth = part_grad.shape[2]
    factor = factor_of(count, tokens, depth)
    step = BLOCK // heads
    share = step * per
    for b in range(0, tok // step, 2):
        both = [
            jnp.concatenate([part_grad[g, (b + i) * share : (b + i + 1) * share, :] for g in range(groups)], axis=0)
            for i in range(2)
        ]
        both = (jnp.concatenate(both, axis=1) * factor).astype(BF16)
        both = dot(unsort[...], both).astype(BF16)
        query_grad[b * BLOCK : (b + 1) * BLOCK, :] = both[:, :depth]
        query_grad[(b + 1) * BLOCK : (b + 2) * BLOCK, :] = both[:, depth:]


def key_kernel(tokens, count, own, back, key_grad):
    factor = factor_of(count, tokens, own.shape[1])
    key_grad[...] = ((own[...] + back[...].astype(F32)) * factor).astype(BF16)


VMEM = pl.BlockSpec(memory_space=pltpu.VMEM)
HBM = pl.BlockSpec(memory_space=pltpu.HBM)


def call(kernel, ins, outs, scratch=()):
    return pl.pallas_call(
        kernel,
        out_shape=[jax.ShapeDtypeStruct(shape, dtype) for shape, dtype in outs],
        in_specs=ins,
        out_specs=[VMEM] * len(outs),
        scratch_shapes=list(scratch),
        compiler_params=pltpu.CompilerParams(vmem_limit_bytes=32 * 1024 * 1024),
    )


def partner(value, axis, hop):
    return lax.ppermute(value, axis, [(i, i ^ hop) for i in range(lax.axis_size(axis))])


def add_partner(value, axis, hop):
    return value + partner(value, axis, hop)


def per_device(query_rows, key_rows, value_matrix, out_grad, offsets, query_head_group):
    _, tok, heads, depth = query_rows.shape
    groups = key_rows.shape[2]
    per = heads // groups
    sizes = (tok, heads, groups, per)
    ctx = lax.axis_size("ctx")
    tokens = float(offsets.shape[0] * lax.axis_size("dp") * tok * ctx)
    ahead = [(i, (i + 1) % ctx) for i in range(ctx)]
    behind = [((i + 1) % ctx, i) for i in range(ctx)]

    back_key = lax.ppermute(key_rows, "ctx", ahead).reshape(tok * groups, depth)
    back_value = lax.ppermute(value_matrix, "ctx", ahead).reshape(tok * groups, depth)
    dp = lax.axis_size("dp")
    paired = dp >= 8 and dp & (dp - 1) == 0
    hops = [1 << i for i in range(dp.bit_length() - 1)] if paired else []
    count = add_partner(offsets, "dp", hops[-1]) if paired else lax.psum(offsets, "dp")

    sorted_shape = (groups, tok * per, depth)
    packed = (tok * groups, depth)
    split = (groups, tok, depth)
    here = BLOCK // per
    sorted_query, sorted_grad, unsort, bias, own_key, own_value = call(
        functools.partial(arrange_kernel, sizes),
        [HBM] * 6,
        [
            (sorted_shape, BF16),
            (sorted_shape, BF16),
            ((BLOCK, BLOCK), BF16),
            ((tok, tok * per), F32),
            (split, BF16),
            (split, BF16),
        ],
        [
            pltpu.SMEM(offsets.shape, jnp.int32),
            pltpu.SMEM((heads,), jnp.int32),
            pltpu.VMEM((tok * heads, depth), BF16),
            pltpu.VMEM((tok * heads, depth), BF16),
            pltpu.VMEM(packed, BF16),
            pltpu.VMEM(packed, BF16),
            pltpu.VMEM(packed, F32),
            pltpu.SemaphoreType.DMA((6,)),
        ],
    )(
        *[
            pltpu.with_memory_space_constraint(x, pltpu.HBM)
            for x in (
                offsets,
                query_head_group,
                query_rows.reshape(tok * heads, depth),
                out_grad.reshape(tok * heads, depth),
                key_rows.reshape(packed),
                value_matrix.reshape(packed),
            )
        ]
    )

    count, unsort = lax.optimization_barrier((count, unsort))
    for hop in hops[2:-1]:
        count = add_partner(count, "dp", hop)
    moved = partner(count, "dp", 1) if paired else count

    probs, back_key = call(
        functools.partial(probs_kernel, sizes),
        [VMEM] * 4,
        [((groups, tok, tok * per), F32), (split, BF16)],
        [pltpu.VMEM(packed, F32)],
    )(bias, sorted_query, own_key, back_key)
    score_grad, own, back = call(
        functools.partial(score_kernel, sizes),
        [VMEM] * 5,
        [((groups, tok // here, tok + here, BLOCK), BF16), (split, F32), (packed, BF16)],
        [pltpu.VMEM(split, BF16), pltpu.VMEM(packed, F32)],
    )(probs, sorted_query, sorted_grad, own_value, back_value)

    moved, back = lax.optimization_barrier((moved, back))
    back = lax.ppermute(back, "ctx", behind)
    if paired:
        count = add_partner(count + moved, "dp", 2)

    part_grad, own = call(
        functools.partial(query_kernel, sizes), [VMEM] * 4, [(sorted_shape, F32), (packed, F32)]
    )(score_grad, own_key, back_key, own)
    (query_grad,) = call(
        functools.partial(unsort_kernel, sizes, tokens), [VMEM] * 3, [((tok * heads, depth), BF16)]
    )(count, part_grad, unsort)
    (key_grad,) = call(
        functools.partial(key_kernel, tokens), [VMEM] * 3, [((tok * groups, depth), BF16)]
    )(count, own, back)
    return (query_grad.reshape(query_rows.shape), key_grad.reshape(key_rows.shape))


def solution(mesh):
    return jax.shard_map(
        per_device,
        mesh=mesh,
        in_specs=(
            P("dp", "ctx", None, None),
            P("dp", "ctx", None, None),
            P("dp", "ctx", None, None),
            P("dp", "ctx", None, None),
            P("dp", None),
            P(),
        ),
        out_specs=(P("dp", "ctx", None, None), P("dp", "ctx", None, None)),
        check_vma=False,
    )
```

```python
import functools
import math

import jax
import jax.numpy as jnp
from jax import lax
from jax.experimental import pallas as pl
from jax.experimental.pallas import tpu as pltpu
from jax.sharding import PartitionSpec as P

NT = (((1,), (1,)), ((), ()))
NN = (((1,), (0,)), ((), ()))
TN = (((0,), (0,)), ((), ()))
F32, BF16 = jnp.float32, jnp.bfloat16
BLOCK = 256


def dot(a, b, dims=NN):
    return lax.dot_general(a, b, dims, preferred_element_type=F32)


def stack(*spans):
    pieces = [v[a:b] for v, a, b in spans if b > a]
    return pieces[0] if len(pieces) == 1 else jnp.concatenate(pieces, axis=0)


def split_heads(packed, flat, out, rows, groups):
    flat[...] = packed[...].astype(F32)
    for g in range(groups):
        out[g] = flat[pl.ds(g, rows, stride=groups), :].astype(BF16)


def place_kernel(sizes, places):
    tok, heads, groups, per = sizes
    shape = (tok, tok * per)
    col = lax.broadcasted_iota(jnp.int32, shape, 0)
    row = lax.broadcasted_iota(jnp.int32, shape, 1) // per
    places[...] = col - jnp.where(col > row, tok, 0)


def plan_kernel(sizes, bounds, group, places, sort, unsort, bias):
    tok, heads, groups, per = sizes
    step = BLOCK // heads
    share = step * per
    first = lax.broadcasted_iota(jnp.int32, (heads, heads), 0)
    second = lax.broadcasted_iota(jnp.int32, (heads, heads), 1)
    along = jnp.broadcast_to(group[...], (heads, heads))
    down = jnp.sum(jnp.where(first == second, along, 0), axis=1, keepdims=True)
    earlier = (first < second) & (down == along)
    slot = group[...] * share + jnp.sum(jnp.where(earlier, 1, 0), axis=0, keepdims=True)
    target = jnp.concatenate([slot + i * per for i in range(step)], axis=1)
    rows = lax.broadcasted_iota(jnp.int32, (BLOCK, BLOCK), 0)
    moves = jnp.where(rows == target, 1.0, 0.0).astype(F32)
    unsort[...] = moves.T.astype(BF16)
    sort[...] = moves.astype(BF16)
    start = lax.axis_index("ctx") * tok
    row = lax.broadcasted_iota(jnp.int32, (8, tok * per), 1) // per
    place = row + start
    low = jnp.zeros_like(place)
    last = bounds.shape[1] - 1
    for i in range(1, last):
        low = jnp.where(place >= bounds[:, i : i + 1], bounds[:, i : i + 1], low)
    low = jnp.where(place >= bounds[:, last : last + 1], jnp.int32(1 << 30), low) - start
    for c in range(0, tok, 8):
        bias[c : c + 8, :] = jnp.where(places[c : c + 8, :] >= low, 0.0, -1e30).astype(F32)


def arrange_kernel(sizes, sort, query, grad, key, value, sorted_query, sorted_grad, own_key, own_value, flat):
    tok, heads, groups, per = sizes
    step = BLOCK // heads
    share = step * per
    depth = query.shape[1]
    for b in range(tok // step):
        part = slice(b * BLOCK, (b + 1) * BLOCK)
        both = jnp.concatenate([query[part, :], grad[part, :]], axis=1)
        both = dot(sort[...], both).astype(BF16)
        for g in range(groups):
            sorted_query[g, b * share : (b + 1) * share, :] = both[g * share : (g + 1) * share, :depth]
            sorted_grad[g, b * share : (b + 1) * share, :] = both[g * share : (g + 1) * share, depth:]
    split_heads(key, flat, own_key, tok, groups)
    split_heads(value, flat, own_value, tok, groups)


def own_mask(per):
    here = BLOCK // per
    shape = (here, BLOCK)
    return lax.broadcasted_iota(jnp.int32, shape, 0) <= lax.broadcasted_iota(jnp.int32, shape, 1) // per


def product(left, right, g, t, rows, own):
    here, tok = own.shape[0], left.shape[1]
    lo, hi = t * here, (t + 1) * here
    a, b = dot(left[g, :hi], rows, NT), dot(right[g, lo:], rows, NT)
    return stack((a, 0, lo), (jnp.where(own, a[lo:], b[:here]), 0, here), (b, here, tok - lo))


def probs_kernel(sizes, bias, query, own_key, back_in, probs, back_key, flat):
    tok, heads, groups, per = sizes
    split_heads(back_in, flat, back_key, tok, groups)
    rate = math.log2(math.e) / math.sqrt(query.shape[2])
    own = own_mask(per)
    for g in range(groups):
        for t in range(tok * per // BLOCK):
            part = slice(t * BLOCK, (t + 1) * BLOCK)
            scores = product(own_key, back_key, g, t, query[g, part, :], own) + bias[:, part]
            top = jnp.maximum(jnp.max(scores, axis=0, keepdims=True), -1e29)
            terms = jnp.exp2((scores - top) * rate)
            scale = 1.0 / jnp.maximum(jnp.sum(terms, axis=0, keepdims=True), 1.0)
            probs[g, :, part] = terms * scale


def score_kernel(sizes, probs, query, grad, own_value, value_in, score_grad, own_grad, back, back_value, flat):
    tok, heads, groups, per = sizes
    split_heads(value_in, flat, back_value, tok, groups)
    here = BLOCK // per
    own = own_mask(per)
    for g in range(groups):
        for t in range(tok // here):
            part = slice(t * BLOCK, (t + 1) * BLOCK)
            lo, hi = t * here, (t + 1) * here
            prob = probs[g, :, part]
            prob_grad = product(own_value, back_value, g, t, grad[g, part, :], own)
            delta = jnp.sum(prob * prob_grad, axis=0, keepdims=True)
            out = prob * (prob_grad - delta)
            mid = out[lo:hi]
            score_grad[g, t, :hi, :] = stack((out, 0, lo), (jnp.where(own, mid, 0.0), 0, here)).astype(BF16)
            score_grad[g, t, hi:, :] = stack((jnp.where(own, 0.0, mid), 0, here), (out, hi, tok)).astype(BF16)
    for g in range(groups):
        own_sum, back_sum = [None] * (tok // here), [None] * (tok // here)
        for t in range(tok // here):
            both = dot(score_grad[g, t], query[g, t * BLOCK : (t + 1) * BLOCK, :])
            for i in range(t + 1):
                piece = both[i * here : (i + 1) * here]
                own_sum[i] = piece if own_sum[i] is None else own_sum[i] + piece
            for i in range(t, tok // here):
                piece = both[(i + 1) * here : (i + 2) * here]
                back_sum[i] = piece if back_sum[i] is None else back_sum[i] + piece
        own_grad[g] = jnp.concatenate(own_sum, axis=0)
        flat[pl.ds(g, tok, stride=groups), :] = jnp.concatenate(back_sum, axis=0)
    back[...] = flat[...].astype(BF16)


def factor_of(count, tokens, depth):
    last = count.shape[1] - 1
    return (tokens / count[0:1, last : last + 1].astype(F32)) * (1.0 / math.sqrt(depth))


def query_kernel(sizes, score_grad, own_key, back_key, own_grad, part_grad, key_grad):
    tok, heads, groups, per = sizes
    here = BLOCK // per
    for g in range(groups):
        for t in range(tok // here):
            keys = jnp.concatenate([own_key[g, : (t + 1) * here], back_key[g, t * here :]], axis=0)
            part_grad[g, t * BLOCK : (t + 1) * BLOCK, :] = dot(score_grad[g, t], keys, TN)
        key_grad[pl.ds(g, tok, stride=groups), :] = own_grad[g]


def unsort_kernel(sizes, tokens, count, part_grad, unsort, query_grad):
    tok, heads, groups, per = sizes
    depth = part_grad.shape[2]
    factor = factor_of(count, tokens, depth)
    step = BLOCK // heads
    share = step * per
    for b in range(0, tok // step, 2):
        both = [
            jnp.concatenate([part_grad[g, (b + i) * share : (b + i + 1) * share, :] for g in range(groups)], axis=0)
            for i in range(2)
        ]
        both = (jnp.concatenate(both, axis=1) * factor).astype(BF16)
        both = dot(unsort[...], both).astype(BF16)
        query_grad[b * BLOCK : (b + 1) * BLOCK, :] = both[:, :depth]
        query_grad[(b + 1) * BLOCK : (b + 2) * BLOCK, :] = both[:, depth:]


def key_kernel(tokens, count, own, back, key_grad):
    factor = factor_of(count, tokens, own.shape[1])
    key_grad[...] = ((own[...] + back[...].astype(F32)) * factor).astype(BF16)


VMEM = pl.BlockSpec(memory_space=pltpu.VMEM)


def call(kernel, ins, outs, scratch=(), flops=None):
    return pl.pallas_call(
        kernel,
        out_shape=[jax.ShapeDtypeStruct(shape, dtype) for shape, dtype in outs],
        in_specs=ins,
        out_specs=[VMEM] * len(outs),
        scratch_shapes=list(scratch),
        cost_estimate=None if flops is None else pl.CostEstimate(flops=flops, bytes_accessed=0, transcendentals=0),
        compiler_params=pltpu.CompilerParams(vmem_limit_bytes=32 * 1024 * 1024),
    )


def partner(value, axis, hop):
    return lax.ppermute(value, axis, [(i, i ^ hop) for i in range(lax.axis_size(axis))])


def add_partner(value, axis, hop):
    return value + partner(value, axis, hop)


def per_device(query_rows, key_rows, value_matrix, out_grad, offsets, query_head_group):
    _, tok, heads, depth = query_rows.shape
    groups = key_rows.shape[2]
    per = heads // groups
    sizes = (tok, heads, groups, per)
    ctx = lax.axis_size("ctx")
    tokens = float(offsets.shape[0] * lax.axis_size("dp") * tok * ctx)
    ahead = [(i, (i + 1) % ctx) for i in range(ctx)]
    behind = [((i + 1) % ctx, i) for i in range(ctx)]

    back_key = lax.ppermute(key_rows, "ctx", ahead).reshape(tok * groups, depth)
    back_value = lax.ppermute(value_matrix, "ctx", ahead).reshape(tok * groups, depth)
    dp = lax.axis_size("dp")
    paired = dp >= 8 and dp & (dp - 1) == 0
    hops = [1 << i for i in range(dp.bit_length() - 1)] if paired else []
    count = add_partner(offsets, "dp", hops[-1]) if paired else lax.psum(offsets, "dp")

    sorted_shape = (groups, tok * per, depth)
    packed = (tok * groups, depth)
    split = (groups, tok, depth)
    here = BLOCK // per
    (places,) = call(functools.partial(place_kernel, sizes), [], [((tok, tok * per), jnp.int32)], flops=1_000_000_000)()
    sort, unsort, bias = call(
        functools.partial(plan_kernel, sizes),
        [VMEM] * 3,
        [((BLOCK, BLOCK), BF16), ((BLOCK, BLOCK), BF16), ((tok, tok * per), F32)],
    )(offsets, query_head_group.reshape(1, heads), places)
    sorted_query, sorted_grad, own_key, own_value = call(
        functools.partial(arrange_kernel, sizes),
        [VMEM] * 5,
        [(sorted_shape, BF16), (sorted_shape, BF16), (split, BF16), (split, BF16)],
        [pltpu.VMEM(packed, F32)],
    )(
        sort,
        query_rows.reshape(tok * heads, depth),
        out_grad.reshape(tok * heads, depth),
        key_rows.reshape(packed),
        value_matrix.reshape(packed),
    )

    count, sorted_query = lax.optimization_barrier((count, sorted_query))
    for hop in hops[2:-1]:
        count = add_partner(count, "dp", hop)
    moved = partner(count, "dp", 1) if paired else count

    probs, back_key = call(
        functools.partial(probs_kernel, sizes),
        [VMEM] * 4,
        [((groups, tok, tok * per), F32), (split, BF16)],
        [pltpu.VMEM(packed, F32)],
    )(bias, sorted_query, own_key, back_key)
    score_grad, own, back = call(
        functools.partial(score_kernel, sizes),
        [VMEM] * 5,
        [((groups, tok // here, tok + here, BLOCK), BF16), (split, F32), (packed, BF16)],
        [pltpu.VMEM(split, BF16), pltpu.VMEM(packed, F32)],
    )(probs, sorted_query, sorted_grad, own_value, back_value)

    moved, back = lax.optimization_barrier((moved, back))
    back = lax.ppermute(back, "ctx", behind)
    if paired:
        count = add_partner(count + moved, "dp", 2)

    part_grad, own = call(
        functools.partial(query_kernel, sizes), [VMEM] * 4, [(sorted_shape, F32), (packed, F32)]
    )(score_grad, own_key, back_key, own)
    (query_grad,) = call(
        functools.partial(unsort_kernel, sizes, tokens), [VMEM] * 3, [((tok * heads, depth), BF16)]
    )(count, part_grad, unsort)
    (key_grad,) = call(
        functools.partial(key_kernel, tokens), [VMEM] * 3, [((tok * groups, depth), BF16)]
    )(count, own, back)
    return (query_grad.reshape(query_rows.shape), key_grad.reshape(key_rows.shape))


def solution(mesh):
    return jax.shard_map(
        per_device,
        mesh=mesh,
        in_specs=(
            P("dp", "ctx", None, None),
            P("dp", "ctx", None, None),
            P("dp", "ctx", None, None),
            P("dp", "ctx", None, None),
            P("dp", None),
            P(),
        ),
        out_specs=(P("dp", "ctx", None, None), P("dp", "ctx", None, None)),
        check_vma=False,
    )
```

```python
import functools
import math

import jax
import jax.numpy as jnp
from jax import lax
from jax.experimental import pallas as pl
from jax.experimental.pallas import tpu as pltpu
from jax.sharding import PartitionSpec as P

NT = (((1,), (1,)), ((), ()))
NN = (((1,), (0,)), ((), ()))
TN = (((0,), (0,)), ((), ()))
F32, BF16 = jnp.float32, jnp.bfloat16
BLOCK = 256
PIECES = 2


def dot(a, b, dims=NN):
    return lax.dot_general(a, b, dims, preferred_element_type=F32)


def stack(*spans):
    pieces = [v[a:b] for v, a, b in spans if b > a]
    return pieces[0] if len(pieces) == 1 else jnp.concatenate(pieces, axis=0)


def split_heads(packed, flat, out, rows, groups):
    flat[...] = packed[...].astype(F32)
    for g in range(groups):
        out[g] = flat[pl.ds(g, rows, stride=groups), :].astype(BF16)


def place_kernel(sizes, places):
    tok, heads, groups, per = sizes
    shape = (tok, tok * per)
    col = lax.broadcasted_iota(jnp.int32, shape, 0)
    row = lax.broadcasted_iota(jnp.int32, shape, 1) // per
    places[...] = col - jnp.where(col > row, tok, 0)


def plan_kernel(sizes, bounds, group, places, sort, unsort, bias):
    tok, heads, groups, per = sizes
    step = BLOCK // heads
    share = step * per
    first = lax.broadcasted_iota(jnp.int32, (heads, heads), 0)
    second = lax.broadcasted_iota(jnp.int32, (heads, heads), 1)
    along = jnp.broadcast_to(group[...], (heads, heads))
    down = jnp.sum(jnp.where(first == second, along, 0), axis=1, keepdims=True)
    earlier = (first < second) & (down == along)
    slot = group[...] * share + jnp.sum(jnp.where(earlier, 1, 0), axis=0, keepdims=True)
    target = jnp.concatenate([slot + i * per for i in range(step)], axis=1)
    rows = lax.broadcasted_iota(jnp.int32, (BLOCK, BLOCK), 0)
    moves = jnp.where(rows == target, 1.0, 0.0).astype(F32)
    unsort[...] = moves.T.astype(BF16)
    sort[...] = moves.astype(BF16)
    start = lax.axis_index("ctx") * tok
    row = lax.broadcasted_iota(jnp.int32, (8, tok * per), 1) // per
    place = row + start
    low = jnp.zeros_like(place)
    last = bounds.shape[1] - 1
    for i in range(1, last):
        low = jnp.where(place >= bounds[:, i : i + 1], bounds[:, i : i + 1], low)
    low = jnp.where(place >= bounds[:, last : last + 1], jnp.int32(1 << 30), low) - start
    for c in range(0, tok, 8):
        bias[c : c + 8, :] = jnp.where(places[c : c + 8, :] >= low, 0.0, -1e30).astype(F32)


def arrange_kernel(sizes, sort, query, grad, key, value, sorted_query, sorted_grad, own_key, own_value, flat):
    tok, heads, groups, per = sizes
    step = BLOCK // heads
    share = step * per
    depth = query.shape[1]
    for b in range(tok // step):
        part = slice(b * BLOCK, (b + 1) * BLOCK)
        both = jnp.concatenate([query[part, :], grad[part, :]], axis=1)
        both = dot(sort[...], both).astype(BF16)
        for g in range(groups):
            sorted_query[g, b * share : (b + 1) * share, :] = both[g * share : (g + 1) * share, :depth]
            sorted_grad[g, b * share : (b + 1) * share, :] = both[g * share : (g + 1) * share, depth:]
    split_heads(key, flat, own_key, tok, groups)
    split_heads(value, flat, own_value, tok, groups)


def own_mask(per):
    here = BLOCK // per
    shape = (here, BLOCK)
    return lax.broadcasted_iota(jnp.int32, shape, 0) <= lax.broadcasted_iota(jnp.int32, shape, 1) // per


def product(left, right, g, t, rows, own):
    here, tok = own.shape[0], left.shape[1]
    lo, hi = t * here, (t + 1) * here
    both = dot(jnp.concatenate([left[g, :hi], right[g, lo:]], axis=0), rows, NT)
    return stack((both, 0, lo), (jnp.where(own, both[lo:hi], both[hi : hi + here]), 0, here), (both, hi + here, tok + here))


def probs_kernel(sizes, bias, query, own_key, back_in, probs, back_key, flat):
    tok, heads, groups, per = sizes
    split_heads(back_in, flat, back_key, tok, groups)
    rate = math.log2(math.e) / math.sqrt(query.shape[2])
    own = own_mask(per)
    for g in range(groups):
        for t in range(tok * per // BLOCK):
            part = slice(t * BLOCK, (t + 1) * BLOCK)
            scores = product(own_key, back_key, g, t, query[g, part, :], own) + bias[:, part]
            top = jnp.maximum(jnp.max(scores, axis=0, keepdims=True), -1e29)
            terms = jnp.exp2((scores - top) * rate)
            scale = 1.0 / jnp.maximum(jnp.sum(terms, axis=0, keepdims=True), 1.0)
            probs[g, :, part] = terms * scale


def score_kernel(sizes, probs, query, grad, own_value, value_in, score_grad, own_grad, back, back_value, flat):
    tok, heads, groups, per = sizes
    split_heads(value_in, flat, back_value, tok, groups)
    here = BLOCK // per
    own = own_mask(per)
    for g in range(groups):
        for t in range(tok // here):
            part = slice(t * BLOCK, (t + 1) * BLOCK)
            lo, hi = t * here, (t + 1) * here
            prob = probs[g, :, part]
            prob_grad = product(own_value, back_value, g, t, grad[g, part, :], own)
            delta = jnp.sum(prob * prob_grad, axis=0, keepdims=True)
            out = prob * (prob_grad - delta)
            mid = out[lo:hi]
            score_grad[g, t, :hi, :] = stack((out, 0, lo), (jnp.where(own, mid, 0.0), 0, here)).astype(BF16)
            score_grad[g, t, hi:, :] = stack((jnp.where(own, 0.0, mid), 0, here), (out, hi, tok)).astype(BF16)
    for g in range(groups):
        own_sum, back_sum = [None] * (tok // here), [None] * (tok // here)
        for t in range(tok // here):
            both = dot(score_grad[g, t], query[g, t * BLOCK : (t + 1) * BLOCK, :])
            for i in range(t + 1):
                piece = both[i * here : (i + 1) * here]
                own_sum[i] = piece if own_sum[i] is None else own_sum[i] + piece
            for i in range(t, tok // here):
                piece = both[(i + 1) * here : (i + 2) * here]
                back_sum[i] = piece if back_sum[i] is None else back_sum[i] + piece
        own_grad[g] = jnp.concatenate(own_sum, axis=0)
        flat[pl.ds(g, tok, stride=groups), :] = jnp.concatenate(back_sum, axis=0)
    back[...] = flat[...].astype(BF16)


def factor_of(count, tokens, depth):
    last = count.shape[1] - 1
    return (tokens / count[0:1, last : last + 1].astype(F32)) * (1.0 / math.sqrt(depth))


def query_kernel(sizes, score_grad, own_key, back_key, own_grad, unsort, query_grad, key_grad, part_grad):
    tok, heads, groups, per = sizes
    depth = own_key.shape[2]
    step = BLOCK // heads
    share = step * per
    here = BLOCK // per
    for g in range(groups):
        for t in range(tok // here):
            keys = jnp.concatenate([own_key[g, : (t + 1) * here], back_key[g, t * here :]], axis=0)
            part_grad[g, t * BLOCK : (t + 1) * BLOCK, :] = dot(score_grad[g, t], keys, TN)
        key_grad[pl.ds(g, tok, stride=groups), :] = own_grad[g]
    for b in range(0, tok // step, 2):
        both = [
            jnp.concatenate([part_grad[g, (b + i) * share : (b + i + 1) * share, :] for g in range(groups)], axis=0)
            for i in range(2)
        ]
        both = jnp.concatenate(both, axis=1)
        high = both.astype(BF16)
        low = (both - high.astype(F32)).astype(BF16)
        both = dot(unsort[...], high) + dot(unsort[...], low)
        query_grad[b * BLOCK : (b + 1) * BLOCK, :] = both[:, :depth]
        query_grad[(b + 1) * BLOCK : (b + 2) * BLOCK, :] = both[:, depth:]


def scale_kernel(tokens, count, query_in, own, back, query_out, key_out, query_grad, key_grad, sems):
    rows, depth = query_in.shape
    last = count.shape[1] - 1
    factor = (tokens / count[0:1, last : last + 1].astype(F32)) * (1.0 / math.sqrt(depth))
    key_grad[...] = ((own[...] + back[...].astype(F32)) * factor).astype(BF16)
    copies = [pltpu.make_async_copy(key_grad, key_out, sems.at[0])]
    copies[0].start()
    for i in range(PIECES):
        part = pl.ds(i * (rows // PIECES), rows // PIECES)
        query_grad[part, :] = (query_in[part, :] * factor).astype(BF16)
        copies.append(pltpu.make_async_copy(query_grad.at[part], query_out.at[part], sems.at[1 + i]))
        copies[-1].start()
    for copy in copies:
        copy.wait()


VMEM = pl.BlockSpec(memory_space=pltpu.VMEM)
HBM = pl.BlockSpec(memory_space=pltpu.HBM)


def call(kernel, ins, outs, scratch=(), flops=None, out_spec=VMEM):
    return pl.pallas_call(
        kernel,
        out_shape=[jax.ShapeDtypeStruct(shape, dtype) for shape, dtype in outs],
        in_specs=ins,
        out_specs=[out_spec] * len(outs),
        scratch_shapes=list(scratch),
        cost_estimate=None if flops is None else pl.CostEstimate(flops=flops, bytes_accessed=0, transcendentals=0),
        compiler_params=pltpu.CompilerParams(vmem_limit_bytes=32 * 1024 * 1024),
    )


def partner(value, axis, hop):
    return lax.ppermute(value, axis, [(i, i ^ hop) for i in range(lax.axis_size(axis))])


def add_partner(value, axis, hop):
    return value + partner(value, axis, hop)


def per_device(query_rows, key_rows, value_matrix, out_grad, offsets, query_head_group):
    _, tok, heads, depth = query_rows.shape
    groups = key_rows.shape[2]
    per = heads // groups
    sizes = (tok, heads, groups, per)
    ctx = lax.axis_size("ctx")
    tokens = float(offsets.shape[0] * lax.axis_size("dp") * tok * ctx)
    ahead = [(i, (i + 1) % ctx) for i in range(ctx)]
    behind = [((i + 1) % ctx, i) for i in range(ctx)]

    back_key = lax.ppermute(key_rows, "ctx", ahead).reshape(tok * groups, depth)
    back_value = lax.ppermute(value_matrix, "ctx", ahead).reshape(tok * groups, depth)
    dp = lax.axis_size("dp")
    paired = dp >= 8 and dp & (dp - 1) == 0
    hops = [1 << i for i in range(dp.bit_length() - 1)] if paired else []
    count = add_partner(offsets, "dp", hops[-1]) if paired else lax.psum(offsets, "dp")

    sorted_shape = (groups, tok * per, depth)
    packed = (tok * groups, depth)
    split = (groups, tok, depth)
    here = BLOCK // per
    (places,) = call(functools.partial(place_kernel, sizes), [], [((tok, tok * per), jnp.int32)], flops=1_000_000_000)()
    sort, unsort, bias = call(
        functools.partial(plan_kernel, sizes),
        [VMEM] * 3,
        [((BLOCK, BLOCK), BF16), ((BLOCK, BLOCK), BF16), ((tok, tok * per), F32)],
    )(offsets, query_head_group.reshape(1, heads), places)
    sorted_query, sorted_grad, own_key, own_value = call(
        functools.partial(arrange_kernel, sizes),
        [VMEM] * 5,
        [(sorted_shape, BF16), (sorted_shape, BF16), (split, BF16), (split, BF16)],
        [pltpu.VMEM(packed, F32)],
    )(
        sort,
        query_rows.reshape(tok * heads, depth),
        out_grad.reshape(tok * heads, depth),
        key_rows.reshape(packed),
        value_matrix.reshape(packed),
    )

    count, sorted_query = lax.optimization_barrier((count, sorted_query))
    for hop in hops[2:-1]:
        count = add_partner(count, "dp", hop)
    moved = partner(count, "dp", 1) if paired else count

    probs, back_key = call(
        functools.partial(probs_kernel, sizes),
        [VMEM] * 4,
        [((groups, tok, tok * per), F32), (split, BF16)],
        [pltpu.VMEM(packed, F32)],
    )(bias, sorted_query, own_key, back_key)
    score_grad, own, back = call(
        functools.partial(score_kernel, sizes),
        [VMEM] * 5,
        [((groups, tok // here, tok + here, BLOCK), BF16), (split, F32), (packed, BF16)],
        [pltpu.VMEM(split, BF16), pltpu.VMEM(packed, F32)],
    )(probs, sorted_query, sorted_grad, own_value, back_value)

    moved, back = lax.optimization_barrier((moved, back))
    back = lax.ppermute(back, "ctx", behind)
    if paired:
        count = add_partner(count + moved, "dp", 2)

    plain_grad, own = call(
        functools.partial(query_kernel, sizes),
        [VMEM] * 5,
        [((tok * heads, depth), F32), (packed, F32)],
        [pltpu.VMEM(sorted_shape, F32)],
    )(score_grad, own_key, back_key, own, unsort)
    query_grad, key_grad = call(
        functools.partial(scale_kernel, tokens),
        [VMEM] * 4,
        [((tok * heads, depth), BF16), (packed, BF16)],
        [
            pltpu.VMEM((tok * heads, depth), BF16),
            pltpu.VMEM(packed, BF16),
            pltpu.SemaphoreType.DMA((1 + PIECES,)),
        ],
        out_spec=HBM,
    )(count, plain_grad, own, back)
    return (query_grad.reshape(query_rows.shape), key_grad.reshape(key_rows.shape))


def solution(mesh):
    return jax.shard_map(
        per_device,
        mesh=mesh,
        in_specs=(
            P("dp", "ctx", None, None),
            P("dp", "ctx", None, None),
            P("dp", "ctx", None, None),
            P("dp", "ctx", None, None),
            P("dp", None),
            P(),
        ),
        out_specs=(P("dp", "ctx", None, None), P("dp", "ctx", None, None)),
        check_vma=False,
    )
```

```python
import functools
import math

import jax
import jax.numpy as jnp
from jax import lax
from jax.experimental import pallas as pl
from jax.experimental.pallas import tpu as pltpu
from jax.sharding import PartitionSpec as P

NT = (((1,), (1,)), ((), ()))
NN = (((1,), (0,)), ((), ()))
TN = (((0,), (0,)), ((), ()))
F32, BF16 = jnp.float32, jnp.bfloat16
BLOCK = 256
PIECES = 2


def dot(a, b, dims=NN):
    return lax.dot_general(a, b, dims, preferred_element_type=F32)


def stack(*spans):
    pieces = [v[a:b] for v, a, b in spans if b > a]
    return pieces[0] if len(pieces) == 1 else jnp.concatenate(pieces, axis=0)


def split_heads(packed, flat, out, rows, groups):
    flat[...] = packed[...].astype(F32)
    for g in range(groups):
        out[g] = flat[pl.ds(g, rows, stride=groups), :].astype(BF16)


def place_kernel(sizes, places):
    tok, heads, groups, per = sizes
    shape = (tok, tok * per)
    col = lax.broadcasted_iota(jnp.int32, shape, 0)
    row = lax.broadcasted_iota(jnp.int32, shape, 1) // per
    places[...] = col - jnp.where(col > row, tok, 0)


def plan_kernel(sizes, bounds, group, places, sort, unsort, bias):
    tok, heads, groups, per = sizes
    step = BLOCK // heads
    share = step * per
    first = lax.broadcasted_iota(jnp.int32, (heads, heads), 0)
    second = lax.broadcasted_iota(jnp.int32, (heads, heads), 1)
    along = jnp.broadcast_to(group[...], (heads, heads))
    down = jnp.sum(jnp.where(first == second, along, 0), axis=1, keepdims=True)
    earlier = (first < second) & (down == along)
    slot = group[...] * share + jnp.sum(jnp.where(earlier, 1, 0), axis=0, keepdims=True)
    target = jnp.concatenate([slot + i * per for i in range(step)], axis=1)
    rows = lax.broadcasted_iota(jnp.int32, (BLOCK, BLOCK), 0)
    moves = jnp.where(rows == target, 1.0, 0.0).astype(F32)
    unsort[...] = moves.T.astype(BF16)
    sort[...] = moves.astype(BF16)
    start = lax.axis_index("ctx") * tok
    row = lax.broadcasted_iota(jnp.int32, (8, tok * per), 1) // per
    place = row + start
    low = jnp.zeros_like(place)
    last = bounds.shape[1] - 1
    for i in range(1, last):
        low = jnp.where(place >= bounds[:, i : i + 1], bounds[:, i : i + 1], low)
    low = jnp.where(place >= bounds[:, last : last + 1], jnp.int32(1 << 30), low) - start
    for c in range(0, tok, 8):
        bias[c : c + 8, :] = jnp.where(places[c : c + 8, :] >= low, 0.0, -1e30).astype(F32)


def arrange_kernel(sizes, sort, query, grad, key, value, sorted_query, sorted_grad, own_key, own_value, flat):
    tok, heads, groups, per = sizes
    step = BLOCK // heads
    share = step * per
    depth = query.shape[1]
    for b in range(tok // step):
        part = slice(b * BLOCK, (b + 1) * BLOCK)
        both = jnp.concatenate([query[part, :], grad[part, :]], axis=1)
        both = dot(sort[...], both).astype(BF16)
        for g in range(groups):
            sorted_query[g, b * share : (b + 1) * share, :] = both[g * share : (g + 1) * share, :depth]
            sorted_grad[g, b * share : (b + 1) * share, :] = both[g * share : (g + 1) * share, depth:]
    split_heads(key, flat, own_key, tok, groups)
    split_heads(value, flat, own_value, tok, groups)


def own_mask(per):
    here = BLOCK // per
    shape = (here, BLOCK)
    return lax.broadcasted_iota(jnp.int32, shape, 0) <= lax.broadcasted_iota(jnp.int32, shape, 1) // per


def merge(left, right, t, own):
    here = own.shape[0]
    lo, hi = t * here, (t + 1) * here
    mid = jnp.where(own, left[lo:hi], right[:here])
    return stack((left, 0, lo), (mid, 0, here), (right, here, right.shape[0]))


def probs_kernel(sizes, bias, query, grad, own_key, own_value, back_in, probs, own_prob_grad, own_delta, back_key, flat):
    tok, heads, groups, per = sizes
    split_heads(back_in, flat, back_key, tok, groups)
    rate = math.log2(math.e) / math.sqrt(query.shape[2])
    own = own_mask(per)
    here = BLOCK // per
    for g in range(groups):
        for t in range(tok // here):
            part = slice(t * BLOCK, (t + 1) * BLOCK)
            lo, hi = t * here, (t + 1) * here
            both = dot(jnp.concatenate([own_key[g, :hi], back_key[g, lo:]], axis=0), query[g, part, :], NT)
            scores = merge(both[:hi], both[hi:], t, own) + bias[:, part]
            top = jnp.maximum(jnp.max(scores, axis=0, keepdims=True), -1e29)
            terms = jnp.exp2((scores - top) * rate)
            scale = 1.0 / jnp.maximum(jnp.sum(terms, axis=0, keepdims=True), 1.0)
            prob = terms * scale
            probs[g, t] = prob
            prob_grad = dot(own_value[g, :hi], grad[g, part, :], NT)
            own_prob_grad[g, t, :hi] = prob_grad
            both = prob[:hi] * prob_grad
            both = stack((both, 0, lo), (jnp.where(own, both[lo:], 0.0), 0, here))
            own_delta[g, t] = jnp.sum(both, axis=0, keepdims=True)


def add_rows(sums, first, piece, here):
    for i in range(piece.shape[0] // here):
        block = piece[i * here : (i + 1) * here]
        sums[first + i] = block if sums[first + i] is None else sums[first + i] + block


def score_kernel(sizes, probs, own_delta, query, grad, value_in, back_score, delta_out, back, back_value, flat):
    tok, heads, groups, per = sizes
    split_heads(value_in, flat, back_value, tok, groups)
    here = BLOCK // per
    own = own_mask(per)
    for g in range(groups):
        for t in range(tok // here):
            lo = t * here
            prob = probs[g, t, lo:]
            prob = stack((jnp.where(own, 0.0, prob[:here]), 0, here), (prob, here, tok - lo))
            prob_grad = dot(back_value[g, lo:], grad[g, t * BLOCK : (t + 1) * BLOCK, :], NT)
            delta = own_delta[g, t] + jnp.sum(prob * prob_grad, axis=0, keepdims=True)
            delta_out[g, t] = delta
            back_score[g, t, lo:] = (prob * (prob_grad - delta)).astype(BF16)
    for g in range(groups):
        sums = [None] * (tok // here)
        for t in range(tok // here):
            rows = query[g, t * BLOCK : (t + 1) * BLOCK, :]
            add_rows(sums, t, dot(back_score[g, t, t * here :, :], rows), here)
        flat[pl.ds(g, tok, stride=groups), :] = jnp.concatenate(sums, axis=0)
    back[...] = flat[...].astype(BF16)


def query_kernel(sizes, probs, own_prob_grad, delta, back_score, query, own_key, back_key, unsort, query_grad, key_grad, part_grad, own_score):
    tok, heads, groups, per = sizes
    depth = own_key.shape[2]
    step = BLOCK // heads
    share = step * per
    here = BLOCK // per
    own = own_mask(per)
    for g in range(groups):
        for t in range(tok // here):
            lo, hi = t * here, (t + 1) * here
            out = probs[g, t, :hi] * (own_prob_grad[g, t, :hi] - delta[g, t])
            own_score[g, t, :hi] = stack((out, 0, lo), (jnp.where(own, out[lo:], 0.0), 0, here)).astype(BF16)
    for g in range(groups):
        for t in range(tok // here):
            lo, hi = t * here, (t + 1) * here
            keys = jnp.concatenate([own_key[g, :hi], back_key[g, lo:]], axis=0)
            both = jnp.concatenate([own_score[g, t, :hi], back_score[g, t, lo:]], axis=0)
            part_grad[g, t * BLOCK : (t + 1) * BLOCK, :] = dot(both, keys, TN)
    for g in range(groups):
        sums = [None] * (tok // here)
        for t in range(tok // here):
            rows = query[g, t * BLOCK : (t + 1) * BLOCK, :]
            add_rows(sums, 0, dot(own_score[g, t, : (t + 1) * here, :], rows), here)
        key_grad[pl.ds(g, tok, stride=groups), :] = jnp.concatenate(sums, axis=0)
    for b in range(0, tok // step, 2):
        both = [
            jnp.concatenate([part_grad[g, (b + i) * share : (b + i + 1) * share, :] for g in range(groups)], axis=0)
            for i in range(2)
        ]
        both = jnp.concatenate(both, axis=1)
        high = both.astype(BF16)
        low = (both - high.astype(F32)).astype(BF16)
        both = dot(unsort[...], high) + dot(unsort[...], low)
        query_grad[b * BLOCK : (b + 1) * BLOCK, :] = both[:, :depth]
        query_grad[(b + 1) * BLOCK : (b + 2) * BLOCK, :] = both[:, depth:]


def scale_kernel(tokens, count, query_in, own, back, query_out, key_out, query_grad, key_grad, sems):
    rows, depth = query_in.shape
    last = count.shape[1] - 1
    factor = (tokens / count[0:1, last : last + 1].astype(F32)) * (1.0 / math.sqrt(depth))
    key_grad[...] = ((own[...] + back[...].astype(F32)) * factor).astype(BF16)
    copies = [pltpu.make_async_copy(key_grad, key_out, sems.at[0])]
    copies[0].start()
    for i in range(PIECES):
        part = pl.ds(i * (rows // PIECES), rows // PIECES)
        query_grad[part, :] = (query_in[part, :] * factor).astype(BF16)
        copies.append(pltpu.make_async_copy(query_grad.at[part], query_out.at[part], sems.at[1 + i]))
        copies[-1].start()
    for copy in copies:
        copy.wait()


VMEM = pl.BlockSpec(memory_space=pltpu.VMEM)
HBM = pl.BlockSpec(memory_space=pltpu.HBM)


def call(kernel, ins, outs, scratch=(), flops=None, out_spec=VMEM):
    return pl.pallas_call(
        kernel,
        out_shape=[jax.ShapeDtypeStruct(shape, dtype) for shape, dtype in outs],
        in_specs=ins,
        out_specs=[out_spec] * len(outs),
        scratch_shapes=list(scratch),
        cost_estimate=None if flops is None else pl.CostEstimate(flops=flops, bytes_accessed=0, transcendentals=0),
        compiler_params=pltpu.CompilerParams(vmem_limit_bytes=32 * 1024 * 1024),
    )


def partner(value, axis, hop):
    return lax.ppermute(value, axis, [(i, i ^ hop) for i in range(lax.axis_size(axis))])


def add_partner(value, axis, hop):
    return value + partner(value, axis, hop)


def per_device(query_rows, key_rows, value_matrix, out_grad, offsets, query_head_group):
    _, tok, heads, depth = query_rows.shape
    groups = key_rows.shape[2]
    per = heads // groups
    sizes = (tok, heads, groups, per)
    ctx = lax.axis_size("ctx")
    tokens = float(offsets.shape[0] * lax.axis_size("dp") * tok * ctx)
    ahead = [(i, (i + 1) % ctx) for i in range(ctx)]
    behind = [((i + 1) % ctx, i) for i in range(ctx)]

    back_key = lax.ppermute(key_rows, "ctx", ahead).reshape(tok * groups, depth)
    back_value = lax.ppermute(value_matrix, "ctx", ahead).reshape(tok * groups, depth)
    dp = lax.axis_size("dp")
    paired = dp >= 8 and dp & (dp - 1) == 0
    hops = [1 << i for i in range(dp.bit_length() - 1)] if paired else []
    moved = partner(offsets, "dp", hops[-1]) if paired else lax.psum(offsets, "dp")

    sorted_shape = (groups, tok * per, depth)
    packed = (tok * groups, depth)
    split = (groups, tok, depth)
    here = BLOCK // per
    (places,) = call(functools.partial(place_kernel, sizes), [], [((tok, tok * per), jnp.int32)], flops=1_000_000_000)()
    sort, unsort, bias = call(
        functools.partial(plan_kernel, sizes),
        [VMEM] * 3,
        [((BLOCK, BLOCK), BF16), ((BLOCK, BLOCK), BF16), ((tok, tok * per), F32)],
    )(offsets, query_head_group.reshape(1, heads), places)
    sorted_query, sorted_grad, own_key, own_value = call(
        functools.partial(arrange_kernel, sizes),
        [VMEM] * 5,
        [(sorted_shape, BF16), (sorted_shape, BF16), (split, BF16), (split, BF16)],
        [pltpu.VMEM(packed, F32)],
    )(
        sort,
        query_rows.reshape(tok * heads, depth),
        out_grad.reshape(tok * heads, depth),
        key_rows.reshape(packed),
        value_matrix.reshape(packed),
    )

    tall = (groups, tok // here, tok, BLOCK)
    line = (groups, tok // here, 1, BLOCK)
    probs, own_prob_grad, own_delta, back_key = call(
        functools.partial(probs_kernel, sizes),
        [VMEM] * 6,
        [(tall, F32), (tall, F32), (line, F32), (split, BF16)],
        [pltpu.VMEM(packed, F32)],
    )(bias, sorted_query, sorted_grad, own_key, own_value, back_key)
    moved, probs = lax.optimization_barrier((moved, probs))
    if paired:
        count = offsets + moved
        for hop in hops[2:-1]:
            count = add_partner(count, "dp", hop)
        moved = partner(count, "dp", 1)
    back_score, delta, back = call(
        functools.partial(score_kernel, sizes),
        [VMEM] * 5,
        [(tall, BF16), (line, F32), (packed, BF16)],
        [pltpu.VMEM(split, BF16), pltpu.VMEM(packed, F32)],
    )(probs, own_delta, sorted_query, sorted_grad, back_value)

    moved, back = lax.optimization_barrier((moved, back))
    back = lax.ppermute(back, "ctx", behind)
    count, delta = lax.optimization_barrier((count + moved, delta)) if paired else (moved, delta)
    count = add_partner(count, "dp", 2) if paired else count

    plain_grad, own = call(
        functools.partial(query_kernel, sizes),
        [VMEM] * 8,
        [((tok * heads, depth), F32), (packed, F32)],
        [pltpu.VMEM(sorted_shape, F32), pltpu.VMEM(tall, BF16)],
    )(probs, own_prob_grad, delta, back_score, sorted_query, own_key, back_key, unsort)
    query_grad, key_grad = call(
        functools.partial(scale_kernel, tokens),
        [VMEM] * 4,
        [((tok * heads, depth), BF16), (packed, BF16)],
        [
            pltpu.VMEM((tok * heads, depth), BF16),
            pltpu.VMEM(packed, BF16),
            pltpu.SemaphoreType.DMA((1 + PIECES,)),
        ],
        out_spec=HBM,
    )(count, plain_grad, own, back)
    return (query_grad.reshape(query_rows.shape), key_grad.reshape(key_rows.shape))


def solution(mesh):
    return jax.shard_map(
        per_device,
        mesh=mesh,
        in_specs=(
            P("dp", "ctx", None, None),
            P("dp", "ctx", None, None),
            P("dp", "ctx", None, None),
            P("dp", "ctx", None, None),
            P("dp", None),
            P(),
        ),
        out_specs=(P("dp", "ctx", None, None), P("dp", "ctx", None, None)),
        check_vma=False,
    )
```

```python
import functools
import math

import jax
import jax.numpy as jnp
from jax import lax
from jax.experimental import pallas as pl
from jax.experimental.pallas import tpu as pltpu
from jax.sharding import PartitionSpec as P

NT = (((1,), (1,)), ((), ()))
NN = (((1,), (0,)), ((), ()))
TN = (((0,), (0,)), ((), ()))
F32, BF16 = jnp.float32, jnp.bfloat16
BLOCK = 256
PIECES = 2


def dot(a, b, dims=NN):
    return lax.dot_general(a, b, dims, preferred_element_type=F32)


def stack(*spans):
    pieces = [v[a:b] for v, a, b in spans if b > a]
    return pieces[0] if len(pieces) == 1 else jnp.concatenate(pieces, axis=0)


def split_heads(packed, flat, out, rows, groups):
    flat[...] = packed[...].astype(F32)
    for g in range(groups):
        out[g] = flat[pl.ds(g, rows, stride=groups), :].astype(BF16)


def place_kernel(sizes, places):
    tok, heads, groups, per = sizes
    shape = (tok, tok * per)
    col = lax.broadcasted_iota(jnp.int32, shape, 0)
    row = lax.broadcasted_iota(jnp.int32, shape, 1) // per
    places[...] = col - jnp.where(col > row, tok, 0)


def plan_kernel(sizes, bounds, group, places, sort, unsort, bias):
    tok, heads, groups, per = sizes
    step = BLOCK // heads
    share = step * per
    first = lax.broadcasted_iota(jnp.int32, (heads, heads), 0)
    second = lax.broadcasted_iota(jnp.int32, (heads, heads), 1)
    along = jnp.broadcast_to(group[...], (heads, heads))
    down = jnp.sum(jnp.where(first == second, along, 0), axis=1, keepdims=True)
    earlier = (first < second) & (down == along)
    slot = group[...] * share + jnp.sum(jnp.where(earlier, 1, 0), axis=0, keepdims=True)
    target = jnp.concatenate([slot + i * per for i in range(step)], axis=1)
    rows = lax.broadcasted_iota(jnp.int32, (BLOCK, BLOCK), 0)
    moves = jnp.where(rows == target, 1.0, 0.0).astype(F32)
    unsort[...] = moves.T.astype(BF16)
    sort[...] = moves.astype(BF16)
    start = lax.axis_index("ctx") * tok
    row = lax.broadcasted_iota(jnp.int32, (8, tok * per), 1) // per
    place = row + start
    low = jnp.zeros_like(place)
    last = bounds.shape[1] - 1
    for i in range(1, last):
        low = jnp.where(place >= bounds[:, i : i + 1], bounds[:, i : i + 1], low)
    low = jnp.where(place >= bounds[:, last : last + 1], jnp.int32(1 << 30), low) - start
    for c in range(0, tok, 8):
        bias[c : c + 8, :] = jnp.where(places[c : c + 8, :] >= low, 0.0, -1e30).astype(F32)


def arrange_kernel(sizes, sort, query, grad, key, value, sorted_query, sorted_grad, own_key, own_value, flat):
    tok, heads, groups, per = sizes
    step = BLOCK // heads
    share = step * per
    depth = query.shape[1]
    for b in range(tok // step):
        part = slice(b * BLOCK, (b + 1) * BLOCK)
        both = jnp.concatenate([query[part, :], grad[part, :]], axis=1)
        both = dot(sort[...], both).astype(BF16)
        for g in range(groups):
            sorted_query[g, b * share : (b + 1) * share, :] = both[g * share : (g + 1) * share, :depth]
            sorted_grad[g, b * share : (b + 1) * share, :] = both[g * share : (g + 1) * share, depth:]
    split_heads(key, flat, own_key, tok, groups)
    split_heads(value, flat, own_value, tok, groups)


def own_mask(per):
    here = BLOCK // per
    shape = (here, BLOCK)
    return lax.broadcasted_iota(jnp.int32, shape, 0) <= lax.broadcasted_iota(jnp.int32, shape, 1) // per


def merge(left, right, t, own):
    here = own.shape[0]
    lo, hi = t * here, (t + 1) * here
    mid = jnp.where(own, left[lo:hi], right[:here])
    return stack((left, 0, lo), (mid, 0, here), (right, here, right.shape[0]))


def probs_kernel(sizes, bias, query, grad, own_key, own_value, back_in, probs, own_prob_grad, own_delta, back_key, flat):
    tok, heads, groups, per = sizes
    split_heads(back_in, flat, back_key, tok, groups)
    rate = math.log2(math.e) / math.sqrt(query.shape[2])
    own = own_mask(per)
    here = BLOCK // per
    for g in range(groups):
        for t in range(tok // here):
            part = slice(t * BLOCK, (t + 1) * BLOCK)
            lo, hi = t * here, (t + 1) * here
            both = dot(jnp.concatenate([own_key[g, :hi], back_key[g, lo:]], axis=0), query[g, part, :], NT)
            scores = merge(both[:hi], both[hi:], t, own) + bias[:, part]
            top = jnp.maximum(jnp.max(scores, axis=0, keepdims=True), -1e29)
            terms = jnp.exp2((scores - top) * rate)
            scale = 1.0 / jnp.maximum(jnp.sum(terms, axis=0, keepdims=True), 1.0)
            prob = terms * scale
            probs[g, t] = prob
            prob_grad = dot(own_value[g, :hi], grad[g, part, :], NT)
            own_prob_grad[g, t, :hi] = prob_grad
            both = prob[:hi] * prob_grad
            both = stack((both, 0, lo), (jnp.where(own, both[lo:], 0.0), 0, here))
            own_delta[g, t] = jnp.sum(both, axis=0, keepdims=True)


def add_rows(sums, first, piece, here):
    for i in range(piece.shape[0] // here):
        block = piece[i * here : (i + 1) * here]
        sums[first + i] = block if sums[first + i] is None else sums[first + i] + block


def score_kernel(sizes, probs, own_delta, query, grad, value_in, back_score, delta_out, back, back_value, flat):
    tok, heads, groups, per = sizes
    split_heads(value_in, flat, back_value, tok, groups)
    here = BLOCK // per
    own = own_mask(per)
    for g in range(groups):
        for t in range(tok // here):
            lo = t * here
            prob = probs[g, t, lo:]
            prob = stack((jnp.where(own, 0.0, prob[:here]), 0, here), (prob, here, tok - lo))
            prob_grad = dot(back_value[g, lo:], grad[g, t * BLOCK : (t + 1) * BLOCK, :], NT)
            delta = own_delta[g, t] + jnp.sum(prob * prob_grad, axis=0, keepdims=True)
            delta_out[g, t] = delta
            back_score[g, t, lo:] = (prob * (prob_grad - delta)).astype(BF16)
    for g in range(groups):
        sums = [None] * (tok // here)
        for t in range(tok // here):
            rows = query[g, t * BLOCK : (t + 1) * BLOCK, :]
            add_rows(sums, t, dot(back_score[g, t, t * here :, :], rows), here)
        flat[pl.ds(g, tok, stride=groups), :] = jnp.concatenate(sums, axis=0)
    back[...] = flat[...].astype(BF16)


def query_kernel(sizes, probs, own_prob_grad, delta, back_score, query, own_key, back_key, unsort, query_grad, key_grad, part_grad, own_score):
    tok, heads, groups, per = sizes
    depth = own_key.shape[2]
    step = BLOCK // heads
    share = step * per
    here = BLOCK // per
    own = own_mask(per)
    for g in range(groups):
        for t in range(tok // here):
            lo, hi = t * here, (t + 1) * here
            out = probs[g, t, :hi] * (own_prob_grad[g, t, :hi] - delta[g, t])
            own_score[g, t, :hi] = stack((out, 0, lo), (jnp.where(own, out[lo:], 0.0), 0, here)).astype(BF16)
    for g in range(groups):
        for t in range(tok // here):
            lo, hi = t * here, (t + 1) * here
            keys = jnp.concatenate([own_key[g, :hi], back_key[g, lo:]], axis=0)
            both = jnp.concatenate([own_score[g, t, :hi], back_score[g, t, lo:]], axis=0)
            part_grad[g, t * BLOCK : (t + 1) * BLOCK, :] = dot(both, keys, TN)
    for g in range(groups):
        sums = [None] * (tok // here)
        for t in range(tok // here):
            rows = query[g, t * BLOCK : (t + 1) * BLOCK, :]
            add_rows(sums, 0, dot(own_score[g, t, : (t + 1) * here, :], rows), here)
        key_grad[pl.ds(g, tok, stride=groups), :] = jnp.concatenate(sums, axis=0)
    for b in range(0, tok // step, 2):
        both = [
            jnp.concatenate([part_grad[g, (b + i) * share : (b + i + 1) * share, :] for g in range(groups)], axis=0)
            for i in range(2)
        ]
        both = jnp.concatenate(both, axis=1)
        high = both.astype(BF16)
        low = (both - high.astype(F32)).astype(BF16)
        both = dot(unsort[...], high) + dot(unsort[...], low)
        query_grad[b * BLOCK : (b + 1) * BLOCK, :] = both[:, :depth]
        query_grad[(b + 1) * BLOCK : (b + 2) * BLOCK, :] = both[:, depth:]


def factor_of(count, tokens, depth):
    last = count.shape[1] - 1
    return (tokens / count[0:1, last : last + 1].astype(F32)) * (1.0 / math.sqrt(depth))


def query_out_kernel(tokens, count, query_in, query_out, query_grad, sems):
    rows, depth = query_in.shape
    factor = factor_of(count, tokens, depth)
    copies = []
    for i in range(PIECES):
        part = pl.ds(i * (rows // PIECES), rows // PIECES)
        query_grad[part, :] = (query_in[part, :] * factor).astype(BF16)
        copies.append(pltpu.make_async_copy(query_grad.at[part], query_out.at[part], sems.at[i]))
        copies[-1].start()
    for copy in copies:
        copy.wait()


def key_out_kernel(tokens, count, own, back, key_grad):
    factor = factor_of(count, tokens, own.shape[1])
    key_grad[...] = ((own[...] + back[...].astype(F32)) * factor).astype(BF16)


VMEM = pl.BlockSpec(memory_space=pltpu.VMEM)
HBM = pl.BlockSpec(memory_space=pltpu.HBM)


def call(kernel, ins, outs, scratch=(), flops=None, out_spec=VMEM):
    return pl.pallas_call(
        kernel,
        out_shape=[jax.ShapeDtypeStruct(shape, dtype) for shape, dtype in outs],
        in_specs=ins,
        out_specs=[out_spec] * len(outs),
        scratch_shapes=list(scratch),
        cost_estimate=None if flops is None else pl.CostEstimate(flops=flops, bytes_accessed=0, transcendentals=0),
        compiler_params=pltpu.CompilerParams(vmem_limit_bytes=32 * 1024 * 1024),
    )


def partner(value, axis, hop):
    return lax.ppermute(value, axis, [(i, i ^ hop) for i in range(lax.axis_size(axis))])


def add_partner(value, axis, hop):
    return value + partner(value, axis, hop)


def per_device(query_rows, key_rows, value_matrix, out_grad, offsets, query_head_group):
    _, tok, heads, depth = query_rows.shape
    groups = key_rows.shape[2]
    per = heads // groups
    sizes = (tok, heads, groups, per)
    ctx = lax.axis_size("ctx")
    tokens = float(offsets.shape[0] * lax.axis_size("dp") * tok * ctx)
    axes, copies = ("ctx", "dp"), lax.axis_size("dp")
    swap = 1 if copies % 2 == 0 else 0
    ahead = [(c * copies + i, (c + 1) * copies + i) for c in range(ctx - 1) for i in range(copies)]
    behind = [(b, a) for a, b in ahead] + [(i ^ swap, (ctx - 1) * copies + i) for i in range(copies)]
    ahead += [((ctx - 1) * copies + i, i) for i in range(copies)]

    back_key = lax.ppermute(key_rows, axes, ahead).reshape(tok * groups, depth)
    back_value = lax.ppermute(value_matrix, axes, ahead).reshape(tok * groups, depth)
    dp = lax.axis_size("dp")
    paired = dp >= 8 and dp & (dp - 1) == 0
    hops = [1 << i for i in range(dp.bit_length() - 1)] if paired else []
    sorted_shape = (groups, tok * per, depth)
    packed = (tok * groups, depth)
    split = (groups, tok, depth)
    here = BLOCK // per
    (places,) = call(functools.partial(place_kernel, sizes), [], [((tok, tok * per), jnp.int32)], flops=1_000_000_000)()
    sort, unsort, bias = call(
        functools.partial(plan_kernel, sizes),
        [VMEM] * 3,
        [((BLOCK, BLOCK), BF16), ((BLOCK, BLOCK), BF16), ((tok, tok * per), F32)],
    )(offsets, query_head_group.reshape(1, heads), places)
    if paired:
        count, sort = lax.optimization_barrier((add_partner(offsets, "dp", 1), sort))
        moved = partner(count, "dp", hops[-1])
    else:
        moved = lax.psum(offsets, "dp")
    sorted_query, sorted_grad, own_key, own_value = call(
        functools.partial(arrange_kernel, sizes),
        [VMEM] * 5,
        [(sorted_shape, BF16), (sorted_shape, BF16), (split, BF16), (split, BF16)],
        [pltpu.VMEM(packed, F32)],
    )(
        sort,
        query_rows.reshape(tok * heads, depth),
        out_grad.reshape(tok * heads, depth),
        key_rows.reshape(packed),
        value_matrix.reshape(packed),
    )

    tall = (groups, tok // here, tok, BLOCK)
    line = (groups, tok // here, 1, BLOCK)
    probs, own_prob_grad, own_delta, back_key = call(
        functools.partial(probs_kernel, sizes),
        [VMEM] * 6,
        [(tall, F32), (tall, F32), (line, F32), (split, BF16)],
        [pltpu.VMEM(packed, F32)],
        500_000_000,
    )(bias, sorted_query, sorted_grad, own_key, own_value, back_key)
    moved, probs = lax.optimization_barrier((moved, probs))
    if paired:
        for hop in hops[2:-1]:
            count = count + moved
            moved = partner(count, "dp", hop)
    back_score, delta, back = call(
        functools.partial(score_kernel, sizes),
        [VMEM] * 5,
        [(tall, BF16), (line, F32), (packed, BF16)],
        [pltpu.VMEM(split, BF16), pltpu.VMEM(packed, F32)],
        2_000_000_000,
    )(probs, own_delta, sorted_query, sorted_grad, back_value)

    moved, back = lax.optimization_barrier((moved, back))
    back = lax.ppermute(back, axes, behind)
    if paired:
        count, delta = lax.optimization_barrier((count + moved, delta))
        count = add_partner(count, "dp", 2)
    else:
        count = moved

    plain_grad, own = call(
        functools.partial(query_kernel, sizes),
        [VMEM] * 8,
        [((tok * heads, depth), F32), (packed, F32)],
        [pltpu.VMEM(sorted_shape, F32), pltpu.VMEM(tall, BF16)],
    )(probs, own_prob_grad, delta, back_score, sorted_query, own_key, back_key, unsort)
    (query_grad,) = call(
        functools.partial(query_out_kernel, tokens),
        [VMEM] * 2,
        [((tok * heads, depth), BF16)],
        [pltpu.VMEM((tok * heads, depth), BF16), pltpu.SemaphoreType.DMA((PIECES,))],
        out_spec=HBM,
    )(count, plain_grad)
    (key_grad,) = call(functools.partial(key_out_kernel, tokens), [VMEM] * 3, [(packed, BF16)])(count, own, back)
    return (query_grad.reshape(query_rows.shape), key_grad.reshape(key_rows.shape))


def solution(mesh):
    return jax.shard_map(
        per_device,
        mesh=mesh,
        in_specs=(
            P("dp", "ctx", None, None),
            P("dp", "ctx", None, None),
            P("dp", "ctx", None, None),
            P("dp", "ctx", None, None),
            P("dp", None),
            P(),
        ),
        out_specs=(P("dp", "ctx", None, None), P("dp", "ctx", None, None)),
        check_vma=False,
    )
```

```python
import functools
import math

import jax
import jax.numpy as jnp
from jax import lax
from jax.experimental import pallas as pl
from jax.experimental.pallas import tpu as pltpu
from jax.sharding import PartitionSpec as P

NT = (((1,), (1,)), ((), ()))
NN = (((1,), (0,)), ((), ()))
TN = (((0,), (0,)), ((), ()))
F32, BF16 = jnp.float32, jnp.bfloat16
BLOCK = 256
PIECES = 4


def dot(a, b, dims=NN):
    return lax.dot_general(a, b, dims, preferred_element_type=F32)


def stack(*spans):
    pieces = [v[a:b] for v, a, b in spans if b > a]
    return pieces[0] if len(pieces) == 1 else jnp.concatenate(pieces, axis=0)


def split_heads(packed, flat, out, rows, groups):
    flat[...] = packed[...].astype(F32)
    for g in range(groups):
        out[g] = flat[pl.ds(g, rows, stride=groups), :].astype(BF16)


def place_kernel(sizes, places):
    tok, heads, groups, per = sizes
    shape = (tok, tok * per)
    col = lax.broadcasted_iota(jnp.int32, shape, 0)
    row = lax.broadcasted_iota(jnp.int32, shape, 1) // per
    places[...] = col - jnp.where(col > row, tok, 0)


def plan_kernel(sizes, bounds, group, places, sort, unsort, bias):
    tok, heads, groups, per = sizes
    step = BLOCK // heads
    share = step * per
    first = lax.broadcasted_iota(jnp.int32, (heads, heads), 0)
    second = lax.broadcasted_iota(jnp.int32, (heads, heads), 1)
    along = jnp.broadcast_to(group[...], (heads, heads))
    down = jnp.sum(jnp.where(first == second, along, 0), axis=1, keepdims=True)
    earlier = (first < second) & (down == along)
    slot = group[...] * share + jnp.sum(jnp.where(earlier, 1, 0), axis=0, keepdims=True)
    target = jnp.concatenate([slot + i * per for i in range(step)], axis=1)
    rows = lax.broadcasted_iota(jnp.int32, (BLOCK, BLOCK), 0)
    moves = jnp.where(rows == target, 1.0, 0.0).astype(F32)
    unsort[...] = moves.T.astype(BF16)
    sort[...] = moves.astype(BF16)
    start = lax.axis_index("ctx") * tok
    row = lax.broadcasted_iota(jnp.int32, (8, tok * per), 1) // per
    place = row + start
    low = jnp.zeros_like(place)
    last = bounds.shape[1] - 1
    for i in range(1, last):
        low = jnp.where(place >= bounds[:, i : i + 1], bounds[:, i : i + 1], low)
    low = jnp.where(place >= bounds[:, last : last + 1], jnp.int32(1 << 30), low) - start
    for c in range(0, tok, 8):
        bias[c : c + 8, :] = jnp.where(places[c : c + 8, :] >= low, 0.0, -1e30).astype(F32)


def arrange_kernel(sizes, sort, query, grad, key, value, sorted_query, sorted_grad, own_key, own_value, flat):
    tok, heads, groups, per = sizes
    step = BLOCK // heads
    share = step * per
    depth = query.shape[1]
    for b in range(tok // step):
        part = slice(b * BLOCK, (b + 1) * BLOCK)
        both = jnp.concatenate([query[part, :], grad[part, :]], axis=1)
        both = dot(sort[...], both).astype(BF16)
        for g in range(groups):
            sorted_query[g, b * share : (b + 1) * share, :] = both[g * share : (g + 1) * share, :depth]
            sorted_grad[g, b * share : (b + 1) * share, :] = both[g * share : (g + 1) * share, depth:]
    split_heads(key, flat, own_key, tok, groups)
    split_heads(value, flat, own_value, tok, groups)


def own_mask(per):
    here = BLOCK // per
    shape = (here, BLOCK)
    return lax.broadcasted_iota(jnp.int32, shape, 0) <= lax.broadcasted_iota(jnp.int32, shape, 1) // per


def merge(left, right, t, own):
    here = own.shape[0]
    lo, hi = t * here, (t + 1) * here
    mid = jnp.where(own, left[lo:hi], right[:here])
    return stack((left, 0, lo), (mid, 0, here), (right, here, right.shape[0]))


def probs_kernel(sizes, bias, query, grad, own_key, own_value, back_in, probs, own_prob_grad, own_delta, back_key, flat):
    tok, heads, groups, per = sizes
    split_heads(back_in, flat, back_key, tok, groups)
    rate = math.log2(math.e) / math.sqrt(query.shape[2])
    own = own_mask(per)
    here = BLOCK // per
    for g in range(groups):
        for t in range(tok // here):
            part = slice(t * BLOCK, (t + 1) * BLOCK)
            lo, hi = t * here, (t + 1) * here
            both = dot(jnp.concatenate([own_key[g, :hi], back_key[g, lo:]], axis=0), query[g, part, :], NT)
            scores = merge(both[:hi], both[hi:], t, own) + bias[:, part]
            top = jnp.maximum(jnp.max(scores, axis=0, keepdims=True), -1e29)
            terms = jnp.exp2((scores - top) * rate)
            scale = 1.0 / jnp.maximum(jnp.sum(terms, axis=0, keepdims=True), 1.0)
            prob = terms * scale
            probs[g, t] = prob
            prob_grad = dot(own_value[g, :hi], grad[g, part, :], NT)
            own_prob_grad[g, t, :hi] = prob_grad
            both = prob[:hi] * prob_grad
            both = stack((both, 0, lo), (jnp.where(own, both[lo:], 0.0), 0, here))
            own_delta[g, t] = jnp.sum(both, axis=0, keepdims=True)


def add_rows(sums, first, piece, here):
    for i in range(piece.shape[0] // here):
        block = piece[i * here : (i + 1) * here]
        sums[first + i] = block if sums[first + i] is None else sums[first + i] + block


def score_kernel(sizes, probs, own_delta, query, grad, value_in, back_score, delta_out, back, back_value, flat):
    tok, heads, groups, per = sizes
    split_heads(value_in, flat, back_value, tok, groups)
    here = BLOCK // per
    own = own_mask(per)
    for g in range(groups):
        for t in range(tok // here):
            lo = t * here
            prob = probs[g, t, lo:]
            prob = stack((jnp.where(own, 0.0, prob[:here]), 0, here), (prob, here, tok - lo))
            prob_grad = dot(back_value[g, lo:], grad[g, t * BLOCK : (t + 1) * BLOCK, :], NT)
            delta = own_delta[g, t] + jnp.sum(prob * prob_grad, axis=0, keepdims=True)
            delta_out[g, t] = delta
            back_score[g, t, lo:] = (prob * (prob_grad - delta)).astype(BF16)
    for g in range(groups):
        sums = [None] * (tok // here)
        for t in range(tok // here):
            rows = query[g, t * BLOCK : (t + 1) * BLOCK, :]
            add_rows(sums, t, dot(back_score[g, t, t * here :, :], rows), here)
        flat[pl.ds(g, tok, stride=groups), :] = jnp.concatenate(sums, axis=0)
    back[...] = flat[...].astype(BF16)


def query_kernel(sizes, probs, own_prob_grad, delta, back_score, query, own_key, back_key, part_grad, key_grad, own_score):
    tok, heads, groups, per = sizes
    here = BLOCK // per
    own = own_mask(per)
    for g in range(groups):
        for t in range(tok // here):
            lo, hi = t * here, (t + 1) * here
            out = probs[g, t, :hi] * (own_prob_grad[g, t, :hi] - delta[g, t])
            own_score[g, t, :hi] = stack((out, 0, lo), (jnp.where(own, out[lo:], 0.0), 0, here)).astype(BF16)
    for g in range(groups):
        for t in range(tok // here):
            lo, hi = t * here, (t + 1) * here
            keys = jnp.concatenate([own_key[g, :hi], back_key[g, lo:]], axis=0)
            both = jnp.concatenate([own_score[g, t, :hi], back_score[g, t, lo:]], axis=0)
            part_grad[g, t * BLOCK : (t + 1) * BLOCK, :] = dot(both, keys, TN)
    for g in range(groups):
        sums = [None] * (tok // here)
        for t in range(tok // here):
            rows = query[g, t * BLOCK : (t + 1) * BLOCK, :]
            add_rows(sums, 0, dot(own_score[g, t, : (t + 1) * here, :], rows), here)
        key_grad[pl.ds(g, tok, stride=groups), :] = jnp.concatenate(sums, axis=0)

def factor_of(count, tokens, depth):
    last = count.shape[1] - 1
    return (tokens / count[0:1, last : last + 1].astype(F32)) * (1.0 / math.sqrt(depth))


def query_out_kernel(sizes, tokens, count, part_grad, unsort, query_out, query_grad, sems):
    tok, heads, groups, per = sizes
    depth = part_grad.shape[2]
    factor = factor_of(count, tokens, depth)
    step = BLOCK // heads
    share = step * per
    rows = tok * heads // PIECES
    copies = []
    for b in range(0, tok // step, 2):
        both = [
            jnp.concatenate([part_grad[g, (b + i) * share : (b + i + 1) * share, :] for g in range(groups)], axis=0)
            for i in range(2)
        ]
        both = (jnp.concatenate(both, axis=1) * factor).astype(BF16)
        both = dot(unsort[...], both).astype(BF16)
        query_grad[b * BLOCK : (b + 1) * BLOCK, :] = both[:, :depth]
        query_grad[(b + 1) * BLOCK : (b + 2) * BLOCK, :] = both[:, depth:]
        done = (b + 2) * BLOCK
        if done % rows == 0:
            part = pl.ds(done - rows, rows)
            copies.append(pltpu.make_async_copy(query_grad.at[part], query_out.at[part], sems.at[len(copies)]))
            copies[-1].start()
    for copy in copies:
        copy.wait()


def key_out_kernel(tokens, count, own, back, key_grad):
    factor = factor_of(count, tokens, own.shape[1])
    key_grad[...] = ((own[...] + back[...].astype(F32)) * factor).astype(BF16)


VMEM = pl.BlockSpec(memory_space=pltpu.VMEM)
HBM = pl.BlockSpec(memory_space=pltpu.HBM)


def call(kernel, ins, outs, scratch=(), flops=None, out_spec=VMEM):
    return pl.pallas_call(
        kernel,
        out_shape=[jax.ShapeDtypeStruct(shape, dtype) for shape, dtype in outs],
        in_specs=ins,
        out_specs=[out_spec] * len(outs),
        scratch_shapes=list(scratch),
        cost_estimate=None if flops is None else pl.CostEstimate(flops=flops, bytes_accessed=0, transcendentals=0),
        compiler_params=pltpu.CompilerParams(vmem_limit_bytes=32 * 1024 * 1024),
    )


def partner(value, axis, hop):
    return lax.ppermute(value, axis, [(i, i ^ hop) for i in range(lax.axis_size(axis))])


def add_partner(value, axis, hop):
    return value + partner(value, axis, hop)


def per_device(query_rows, key_rows, value_matrix, out_grad, offsets, query_head_group):
    _, tok, heads, depth = query_rows.shape
    groups = key_rows.shape[2]
    per = heads // groups
    sizes = (tok, heads, groups, per)
    ctx = lax.axis_size("ctx")
    tokens = float(offsets.shape[0] * lax.axis_size("dp") * tok * ctx)
    axes, copies = ("ctx", "dp"), lax.axis_size("dp")
    swap = 1 if copies % 2 == 0 else 0
    ahead = [(c * copies + i, (c + 1) * copies + i) for c in range(ctx - 1) for i in range(copies)]
    behind = [(b, a) for a, b in ahead] + [(i ^ swap, (ctx - 1) * copies + i) for i in range(copies)]
    keys_ahead = ahead + [((ctx - 1) * copies + i, i ^ swap) for i in range(copies)]
    ahead += [((ctx - 1) * copies + i, i) for i in range(copies)]

    back_key = lax.ppermute(key_rows, axes, keys_ahead).reshape(tok * groups, depth)
    back_value = lax.ppermute(value_matrix, axes, ahead).reshape(tok * groups, depth)
    dp = lax.axis_size("dp")
    paired = dp >= 8 and dp & (dp - 1) == 0
    hops = [1 << i for i in range(dp.bit_length() - 1)] if paired else []
    sorted_shape = (groups, tok * per, depth)
    packed = (tok * groups, depth)
    split = (groups, tok, depth)
    here = BLOCK // per
    (places,) = call(functools.partial(place_kernel, sizes), [], [((tok, tok * per), jnp.int32)], flops=1_000_000_000)()
    sort, unsort, bias = call(
        functools.partial(plan_kernel, sizes),
        [VMEM] * 3,
        [((BLOCK, BLOCK), BF16), ((BLOCK, BLOCK), BF16), ((tok, tok * per), F32)],
    )(offsets, query_head_group.reshape(1, heads), places)
    if paired:
        count, sort = lax.optimization_barrier((add_partner(offsets, "dp", 1), sort))
        moved = partner(count, "dp", hops[-1])
    else:
        moved = lax.psum(offsets, "dp")
    sorted_query, sorted_grad, own_key, own_value = call(
        functools.partial(arrange_kernel, sizes),
        [VMEM] * 5,
        [(sorted_shape, BF16), (sorted_shape, BF16), (split, BF16), (split, BF16)],
        [pltpu.VMEM(packed, F32)],
    )(
        sort,
        query_rows.reshape(tok * heads, depth),
        out_grad.reshape(tok * heads, depth),
        key_rows.reshape(packed),
        value_matrix.reshape(packed),
    )

    tall = (groups, tok // here, tok, BLOCK)
    line = (groups, tok // here, 1, BLOCK)
    probs, own_prob_grad, own_delta, back_key = call(
        functools.partial(probs_kernel, sizes),
        [VMEM] * 6,
        [(tall, F32), (tall, F32), (line, F32), (split, BF16)],
        [pltpu.VMEM(packed, F32)],
        500_000_000,
    )(bias, sorted_query, sorted_grad, own_key, own_value, back_key)
    moved, probs = lax.optimization_barrier((moved, probs))
    if paired:
        for hop in hops[2:-1]:
            count = count + moved
            moved = partner(count, "dp", hop)
    back_score, delta, back = call(
        functools.partial(score_kernel, sizes),
        [VMEM] * 5,
        [(tall, BF16), (line, F32), (packed, BF16)],
        [pltpu.VMEM(split, BF16), pltpu.VMEM(packed, F32)],
        2_000_000_000,
    )(probs, own_delta, sorted_query, sorted_grad, back_value)

    moved, back = lax.optimization_barrier((moved, back))
    back = lax.ppermute(back, axes, behind)
    if paired:
        count, delta = lax.optimization_barrier((count + moved, delta))
        count = add_partner(count, "dp", 2)
    else:
        count = moved

    part_grad, own = call(
        functools.partial(query_kernel, sizes),
        [VMEM] * 7,
        [(sorted_shape, F32), (packed, F32)],
        [pltpu.VMEM(tall, BF16)],
    )(probs, own_prob_grad, delta, back_score, sorted_query, own_key, back_key)
    (query_grad,) = call(
        functools.partial(query_out_kernel, sizes, tokens),
        [VMEM] * 3,
        [((tok * heads, depth), BF16)],
        [pltpu.VMEM((tok * heads, depth), BF16), pltpu.SemaphoreType.DMA((PIECES,))],
        out_spec=HBM,
    )(count, part_grad, unsort)
    (key_grad,) = call(functools.partial(key_out_kernel, tokens), [VMEM] * 3, [(packed, BF16)])(count, own, back)
    return (query_grad.reshape(query_rows.shape), key_grad.reshape(key_rows.shape))


def solution(mesh):
    return jax.shard_map(
        per_device,
        mesh=mesh,
        in_specs=(
            P("dp", "ctx", None, None),
            P("dp", "ctx", None, None),
            P("dp", "ctx", None, None),
            P("dp", "ctx", None, None),
            P("dp", None),
            P(),
        ),
        out_specs=(P("dp", "ctx", None, None), P("dp", "ctx", None, None)),
        check_vma=False,
    )
```

```python
import functools
import math

import jax
import jax.numpy as jnp
from jax import lax
from jax.experimental import pallas as pl
from jax.experimental.pallas import tpu as pltpu
from jax.sharding import PartitionSpec as P

NT = (((1,), (1,)), ((), ()))
NN = (((1,), (0,)), ((), ()))
TN = (((0,), (0,)), ((), ()))
F32, BF16 = jnp.float32, jnp.bfloat16
BLOCK = 256
PIECES = 4


def dot(a, b, dims=NN):
    return lax.dot_general(a, b, dims, preferred_element_type=F32)


def stack(*spans):
    pieces = [v[a:b] for v, a, b in spans if b > a]
    return pieces[0] if len(pieces) == 1 else jnp.concatenate(pieces, axis=0)


def split_heads(packed, flat, out, rows, groups):
    flat[...] = packed[...].astype(F32)
    for g in range(groups):
        out[g] = flat[pl.ds(g, rows, stride=groups), :].astype(BF16)


def place_kernel(sizes, places):
    tok, heads, groups, per = sizes
    shape = (tok, tok * per)
    col = lax.broadcasted_iota(jnp.int32, shape, 0)
    row = lax.broadcasted_iota(jnp.int32, shape, 1) // per
    places[...] = col - jnp.where(col > row, tok, 0)


def plan_kernel(sizes, bounds, group, places, sort, unsort, bias):
    tok, heads, groups, per = sizes
    step = BLOCK // heads
    share = step * per
    first = lax.broadcasted_iota(jnp.int32, (heads, heads), 0)
    second = lax.broadcasted_iota(jnp.int32, (heads, heads), 1)
    along = jnp.broadcast_to(group[...], (heads, heads))
    down = jnp.sum(jnp.where(first == second, along, 0), axis=1, keepdims=True)
    earlier = (first < second) & (down == along)
    slot = group[...] * share + jnp.sum(jnp.where(earlier, 1, 0), axis=0, keepdims=True)
    target = jnp.concatenate([slot + i * per for i in range(step)], axis=1)
    rows = lax.broadcasted_iota(jnp.int32, (BLOCK, BLOCK), 0)
    moves = jnp.where(rows == target, 1.0, 0.0).astype(F32)
    unsort[...] = moves.T.astype(BF16)
    sort[...] = moves.astype(BF16)
    start = lax.axis_index("ctx") * tok
    row = lax.broadcasted_iota(jnp.int32, (8, tok * per), 1) // per
    place = row + start
    low = jnp.zeros_like(place)
    last = bounds.shape[1] - 1
    for i in range(1, last):
        low = jnp.where(place >= bounds[:, i : i + 1], bounds[:, i : i + 1], low)
    low = jnp.where(place >= bounds[:, last : last + 1], jnp.int32(1 << 30), low) - start
    for c in range(0, tok, 8):
        bias[c : c + 8, :] = jnp.where(places[c : c + 8, :] >= low, 0.0, -1e30).astype(F32)


def arrange_kernel(sizes, sort, query, grad, key, value, sorted_query, sorted_grad, own_key, own_value, flat):
    tok, heads, groups, per = sizes
    step = BLOCK // heads
    share = step * per
    depth = query.shape[1]
    for b in range(tok // step):
        part = slice(b * BLOCK, (b + 1) * BLOCK)
        both = jnp.concatenate([query[part, :], grad[part, :]], axis=1)
        both = dot(sort[...], both).astype(BF16)
        for g in range(groups):
            sorted_query[g, b * share : (b + 1) * share, :] = both[g * share : (g + 1) * share, :depth]
            sorted_grad[g, b * share : (b + 1) * share, :] = both[g * share : (g + 1) * share, depth:]
    split_heads(key, flat, own_key, tok, groups)
    split_heads(value, flat, own_value, tok, groups)


def own_mask(per):
    here = BLOCK // per
    shape = (here, BLOCK)
    return lax.broadcasted_iota(jnp.int32, shape, 0) <= lax.broadcasted_iota(jnp.int32, shape, 1) // per


def merge(left, right, t, own):
    here = own.shape[0]
    lo, hi = t * here, (t + 1) * here
    mid = jnp.where(own, left[lo:hi], right[:here])
    return stack((left, 0, lo), (mid, 0, here), (right, here, right.shape[0]))


def probs_kernel(sizes, bias, query, grad, own_key, own_value, back_in, probs, own_prob_grad, own_delta, back_key, flat):
    tok, heads, groups, per = sizes
    split_heads(back_in, flat, back_key, tok, groups)
    rate = math.log2(math.e) / math.sqrt(query.shape[2])
    own = own_mask(per)
    here = BLOCK // per
    for g in range(groups):
        for t in range(tok // here):
            part = slice(t * BLOCK, (t + 1) * BLOCK)
            lo, hi = t * here, (t + 1) * here
            both = dot(jnp.concatenate([own_key[g, :hi], back_key[g, lo:]], axis=0), query[g, part, :], NT)
            scores = merge(both[:hi], both[hi:], t, own) + bias[:, part]
            top = jnp.maximum(jnp.max(scores, axis=0, keepdims=True), -1e29)
            terms = jnp.exp2((scores - top) * rate)
            scale = 1.0 / jnp.maximum(jnp.sum(terms, axis=0, keepdims=True), 1.0)
            prob = terms * scale
            probs[g, t] = prob
            prob_grad = dot(own_value[g, :hi], grad[g, part, :], NT)
            own_prob_grad[g, t, :hi] = prob_grad
            both = prob[:hi] * prob_grad
            both = stack((both, 0, lo), (jnp.where(own, both[lo:], 0.0), 0, here))
            own_delta[g, t] = jnp.sum(both, axis=0, keepdims=True)


def add_rows(sums, first, piece, here):
    for i in range(piece.shape[0] // here):
        block = piece[i * here : (i + 1) * here]
        sums[first + i] = block if sums[first + i] is None else sums[first + i] + block


def score_kernel(sizes, probs, own_delta, query, grad, value_in, back_score, delta_out, back, back_value, flat):
    tok, heads, groups, per = sizes
    split_heads(value_in, flat, back_value, tok, groups)
    here = BLOCK // per
    own = own_mask(per)
    for g in range(groups):
        for t in range(tok // here):
            lo = t * here
            prob = probs[g, t, lo:]
            prob = stack((jnp.where(own, 0.0, prob[:here]), 0, here), (prob, here, tok - lo))
            prob_grad = dot(back_value[g, lo:], grad[g, t * BLOCK : (t + 1) * BLOCK, :], NT)
            delta = own_delta[g, t] + jnp.sum(prob * prob_grad, axis=0, keepdims=True)
            delta_out[g, t] = delta
            back_score[g, t, lo:] = (prob * (prob_grad - delta)).astype(BF16)
    for g in range(groups):
        sums = [None] * (tok // here)
        for t in range(tok // here):
            rows = query[g, t * BLOCK : (t + 1) * BLOCK, :]
            add_rows(sums, t, dot(back_score[g, t, t * here :, :], rows), here)
        flat[pl.ds(g, tok, stride=groups), :] = jnp.concatenate(sums, axis=0)
    back[...] = flat[...].astype(BF16)


def query_kernel(sizes, probs, own_prob_grad, delta, back_score, query, own_key, back_key, unsort, query_grad, key_grad, part_grad, own_score):
    tok, heads, groups, per = sizes
    depth = own_key.shape[2]
    step = BLOCK // heads
    share = step * per
    here = BLOCK // per
    own = own_mask(per)
    for g in range(groups):
        for t in range(tok // here):
            lo, hi = t * here, (t + 1) * here
            out = probs[g, t, :hi] * (own_prob_grad[g, t, :hi] - delta[g, t])
            own_score[g, t, :hi] = stack((out, 0, lo), (jnp.where(own, out[lo:], 0.0), 0, here)).astype(BF16)
    for g in range(groups):
        for t in range(tok // here):
            lo, hi = t * here, (t + 1) * here
            keys = jnp.concatenate([own_key[g, :hi], back_key[g, lo:]], axis=0)
            both = jnp.concatenate([own_score[g, t, :hi], back_score[g, t, lo:]], axis=0)
            part_grad[g, t * BLOCK : (t + 1) * BLOCK, :] = dot(both, keys, TN)
    for g in range(groups):
        sums = [None] * (tok // here)
        for t in range(tok // here):
            rows = query[g, t * BLOCK : (t + 1) * BLOCK, :]
            add_rows(sums, 0, dot(own_score[g, t, : (t + 1) * here, :], rows), here)
        key_grad[pl.ds(g, tok, stride=groups), :] = jnp.concatenate(sums, axis=0)
    for b in range(0, tok // step, 2):
        both = [
            jnp.concatenate([part_grad[g, (b + i) * share : (b + i + 1) * share, :] for g in range(groups)], axis=0)
            for i in range(2)
        ]
        both = jnp.concatenate(both, axis=1)
        high = both.astype(BF16)
        low = (both - high.astype(F32)).astype(BF16)
        both = dot(unsort[...], high) + dot(unsort[...], low)
        query_grad[b * BLOCK : (b + 1) * BLOCK, :] = both[:, :depth]
        query_grad[(b + 1) * BLOCK : (b + 2) * BLOCK, :] = both[:, depth:]


def factor_of(count, tokens, depth):
    last = count.shape[1] - 1
    return (tokens / count[0:1, last : last + 1].astype(F32)) * (1.0 / math.sqrt(depth))


def query_out_kernel(tokens, count, query_in, query_out, factor_out, query_grad, sems):
    rows, depth = query_in.shape
    factor = factor_of(count, tokens, depth)
    factor_out[...] = jnp.broadcast_to(factor, factor_out.shape)
    copies = []
    for i in range(PIECES):
        part = pl.ds(i * (rows // PIECES), rows // PIECES)
        query_grad[part, :] = (query_in[part, :] * factor).astype(BF16)
        copies.append(pltpu.make_async_copy(query_grad.at[part], query_out.at[part], sems.at[i]))
        copies[-1].start()
    for copy in copies:
        copy.wait()


VMEM = pl.BlockSpec(memory_space=pltpu.VMEM)
HBM = pl.BlockSpec(memory_space=pltpu.HBM)


def call(kernel, ins, outs, scratch=(), flops=None, out_spec=VMEM):
    return pl.pallas_call(
        kernel,
        out_shape=[jax.ShapeDtypeStruct(shape, dtype) for shape, dtype in outs],
        in_specs=ins,
        out_specs=out_spec if isinstance(out_spec, list) else [out_spec] * len(outs),
        scratch_shapes=list(scratch),
        cost_estimate=None if flops is None else pl.CostEstimate(flops=flops, bytes_accessed=0, transcendentals=0),
        compiler_params=pltpu.CompilerParams(vmem_limit_bytes=32 * 1024 * 1024),
    )


def partner(value, axis, hop):
    return lax.ppermute(value, axis, [(i, i ^ hop) for i in range(lax.axis_size(axis))])


def add_partner(value, axis, hop):
    return value + partner(value, axis, hop)


def per_device(query_rows, key_rows, value_matrix, out_grad, offsets, query_head_group):
    _, tok, heads, depth = query_rows.shape
    groups = key_rows.shape[2]
    per = heads // groups
    sizes = (tok, heads, groups, per)
    ctx = lax.axis_size("ctx")
    tokens = float(offsets.shape[0] * lax.axis_size("dp") * tok * ctx)
    axes, copies = ("ctx", "dp"), lax.axis_size("dp")
    swap = 1 if copies % 2 == 0 else 0
    ahead = [(c * copies + i, (c + 1) * copies + i) for c in range(ctx - 1) for i in range(copies)]
    behind = [(b, a) for a, b in ahead] + [(i ^ swap, (ctx - 1) * copies + i) for i in range(copies)]
    keys_ahead = ahead + [((ctx - 1) * copies + i, i ^ swap) for i in range(copies)]
    ahead = ahead + [((ctx - 1) * copies + i, i) for i in range(copies)]

    back_key = lax.ppermute(key_rows, axes, keys_ahead).reshape(tok * groups, depth)
    back_value = lax.ppermute(value_matrix, axes, ahead).reshape(tok * groups, depth)
    dp = lax.axis_size("dp")
    paired = dp >= 8 and dp & (dp - 1) == 0
    hops = [1 << i for i in range(dp.bit_length() - 1)] if paired else []
    sorted_shape = (groups, tok * per, depth)
    packed = (tok * groups, depth)
    split = (groups, tok, depth)
    here = BLOCK // per
    (places,) = call(functools.partial(place_kernel, sizes), [], [((tok, tok * per), jnp.int32)], flops=1_000_000_000)()
    sort, unsort, bias = call(
        functools.partial(plan_kernel, sizes),
        [VMEM] * 3,
        [((BLOCK, BLOCK), BF16), ((BLOCK, BLOCK), BF16), ((tok, tok * per), F32)],
    )(offsets, query_head_group.reshape(1, heads), places)
    if paired:
        count, sort = lax.optimization_barrier((add_partner(offsets, "dp", 1), sort))
        moved = partner(count, "dp", hops[-1])
    else:
        moved = lax.psum(offsets, "dp")
    sorted_query, sorted_grad, own_key, own_value = call(
        functools.partial(arrange_kernel, sizes),
        [VMEM] * 5,
        [(sorted_shape, BF16), (sorted_shape, BF16), (split, BF16), (split, BF16)],
        [pltpu.VMEM(packed, F32)],
    )(
        sort,
        query_rows.reshape(tok * heads, depth),
        out_grad.reshape(tok * heads, depth),
        key_rows.reshape(packed),
        value_matrix.reshape(packed),
    )

    tall = (groups, tok // here, tok, BLOCK)
    line = (groups, tok // here, 1, BLOCK)
    probs, own_prob_grad, own_delta, back_key = call(
        functools.partial(probs_kernel, sizes),
        [VMEM] * 6,
        [(tall, F32), (tall, F32), (line, F32), (split, BF16)],
        [pltpu.VMEM(packed, F32)],
        500_000_000,
    )(bias, sorted_query, sorted_grad, own_key, own_value, back_key)
    moved, probs = lax.optimization_barrier((moved, probs))
    if paired:
        for hop in hops[2:-1]:
            count = count + moved
            moved = partner(count, "dp", hop)
    back_score, delta, back = call(
        functools.partial(score_kernel, sizes),
        [VMEM] * 5,
        [(tall, BF16), (line, F32), (packed, BF16)],
        [pltpu.VMEM(split, BF16), pltpu.VMEM(packed, F32)],
        2_000_000_000,
    )(probs, own_delta, sorted_query, sorted_grad, back_value)

    moved, back = lax.optimization_barrier((moved, back))
    back = lax.ppermute(back, axes, behind)
    if paired:
        count, delta = lax.optimization_barrier((count + moved, delta))
        count = add_partner(count, "dp", 2)
    else:
        count = moved

    plain_grad, own = call(
        functools.partial(query_kernel, sizes),
        [VMEM] * 8,
        [((tok * heads, depth), F32), (packed, F32)],
        [pltpu.VMEM(sorted_shape, F32), pltpu.VMEM(tall, BF16)],
    )(probs, own_prob_grad, delta, back_score, sorted_query, own_key, back_key, unsort)
    query_grad, factor = call(
        functools.partial(query_out_kernel, tokens),
        [VMEM] * 2,
        [((tok * heads, depth), BF16), ((1, depth), F32)],
        [pltpu.VMEM((tok * heads, depth), BF16), pltpu.SemaphoreType.DMA((PIECES,))],
        out_spec=[HBM, VMEM],
    )(count, plain_grad)
    key_grad = ((own + back.astype(F32)) * factor).astype(BF16)
    return (query_grad.reshape(query_rows.shape), key_grad.reshape(key_rows.shape))


def solution(mesh):
    return jax.shard_map(
        per_device,
        mesh=mesh,
        in_specs=(
            P("dp", "ctx", None, None),
            P("dp", "ctx", None, None),
            P("dp", "ctx", None, None),
            P("dp", "ctx", None, None),
            P("dp", None),
            P(),
        ),
        out_specs=(P("dp", "ctx", None, None), P("dp", "ctx", None, None)),
        check_vma=False,
    )
```

```python
import functools
import math

import jax
import jax.numpy as jnp
from jax import lax
from jax.experimental import pallas as pl
from jax.experimental.pallas import tpu as pltpu
from jax.sharding import PartitionSpec as P

NT = (((1,), (1,)), ((), ()))
NN = (((1,), (0,)), ((), ()))
TN = (((0,), (0,)), ((), ()))
F32, BF16 = jnp.float32, jnp.bfloat16
BLOCK = 256
PIECES = 4


def dot(a, b, dims=NN):
    return lax.dot_general(a, b, dims, preferred_element_type=F32)


def stack(*spans):
    pieces = [v[a:b] for v, a, b in spans if b > a]
    return pieces[0] if len(pieces) == 1 else jnp.concatenate(pieces, axis=0)


def split_heads(packed, flat, out, rows, groups):
    flat[...] = packed[...].astype(F32)
    for g in range(groups):
        out[g] = flat[pl.ds(g, rows, stride=groups), :].astype(BF16)


def place_kernel(sizes, places):
    tok, heads, groups, per = sizes
    shape = (tok, tok * per)
    col = lax.broadcasted_iota(jnp.int32, shape, 0)
    row = lax.broadcasted_iota(jnp.int32, shape, 1) // per
    places[...] = col - jnp.where(col > row, tok, 0)


def plan_kernel(sizes, bounds, group, places, sort, unsort, bias):
    tok, heads, groups, per = sizes
    step = BLOCK // heads
    share = step * per
    first = lax.broadcasted_iota(jnp.int32, (heads, heads), 0)
    second = lax.broadcasted_iota(jnp.int32, (heads, heads), 1)
    along = jnp.broadcast_to(group[...], (heads, heads))
    down = jnp.sum(jnp.where(first == second, along, 0), axis=1, keepdims=True)
    earlier = (first < second) & (down == along)
    slot = group[...] * share + jnp.sum(jnp.where(earlier, 1, 0), axis=0, keepdims=True)
    target = jnp.concatenate([slot + i * per for i in range(step)], axis=1)
    rows = lax.broadcasted_iota(jnp.int32, (BLOCK, BLOCK), 0)
    moves = jnp.where(rows == target, 1.0, 0.0).astype(F32)
    unsort[...] = moves.T.astype(BF16)
    sort[...] = moves.astype(BF16)
    start = lax.axis_index("ctx") * tok
    row = lax.broadcasted_iota(jnp.int32, (8, tok * per), 1) // per
    place = row + start
    low = jnp.zeros_like(place)
    last = bounds.shape[1] - 1
    for i in range(1, last):
        low = jnp.where(place >= bounds[:, i : i + 1], bounds[:, i : i + 1], low)
    low = jnp.where(place >= bounds[:, last : last + 1], jnp.int32(1 << 30), low) - start
    for c in range(0, tok, 8):
        bias[c : c + 8, :] = jnp.where(places[c : c + 8, :] >= low, 0.0, -1e30).astype(F32)


def arrange_kernel(sizes, sort, query, grad, key, value, sorted_query, sorted_grad, own_key, own_value, flat):
    tok, heads, groups, per = sizes
    step = BLOCK // heads
    share = step * per
    depth = query.shape[1]
    for b in range(tok // step):
        part = slice(b * BLOCK, (b + 1) * BLOCK)
        both = jnp.concatenate([query[part, :], grad[part, :]], axis=1)
        both = dot(sort[...], both).astype(BF16)
        for g in range(groups):
            sorted_query[g, b * share : (b + 1) * share, :] = both[g * share : (g + 1) * share, :depth]
            sorted_grad[g, b * share : (b + 1) * share, :] = both[g * share : (g + 1) * share, depth:]
    split_heads(key, flat, own_key, tok, groups)
    split_heads(value, flat, own_value, tok, groups)


def own_mask(per):
    here = BLOCK // per
    shape = (here, BLOCK)
    return lax.broadcasted_iota(jnp.int32, shape, 0) <= lax.broadcasted_iota(jnp.int32, shape, 1) // per


def merge(left, right, t, own):
    here = own.shape[0]
    lo, hi = t * here, (t + 1) * here
    mid = jnp.where(own, left[lo:hi], right[:here])
    return stack((left, 0, lo), (mid, 0, here), (right, here, right.shape[0]))


def probs_kernel(sizes, bias, query, grad, own_key, own_value, back_in, probs, own_prob_grad, own_delta, back_key, flat):
    tok, heads, groups, per = sizes
    split_heads(back_in, flat, back_key, tok, groups)
    rate = math.log2(math.e) / math.sqrt(query.shape[2])
    own = own_mask(per)
    here = BLOCK // per
    for g in range(groups):
        for t in range(tok // here):
            part = slice(t * BLOCK, (t + 1) * BLOCK)
            lo, hi = t * here, (t + 1) * here
            both = dot(jnp.concatenate([own_key[g, :hi], back_key[g, lo:]], axis=0), query[g, part, :], NT)
            scores = merge(both[:hi], both[hi:], t, own) + bias[:, part]
            top = jnp.maximum(jnp.max(scores, axis=0, keepdims=True), -1e29)
            terms = jnp.exp2((scores - top) * rate)
            scale = 1.0 / jnp.maximum(jnp.sum(terms, axis=0, keepdims=True), 1.0)
            prob = terms * scale
            probs[g, t] = prob
            prob_grad = dot(own_value[g, :hi], grad[g, part, :], NT)
            own_prob_grad[g, t, :hi] = prob_grad
            both = prob[:hi] * prob_grad
            both = stack((both, 0, lo), (jnp.where(own, both[lo:], 0.0), 0, here))
            own_delta[g, t] = jnp.sum(both, axis=0, keepdims=True)


def add_rows(sums, first, piece, here):
    for i in range(piece.shape[0] // here):
        block = piece[i * here : (i + 1) * here]
        sums[first + i] = block if sums[first + i] is None else sums[first + i] + block


def score_kernel(sizes, probs, own_delta, query, grad, value_in, back_score, delta_out, back, back_value, flat):
    tok, heads, groups, per = sizes
    split_heads(value_in, flat, back_value, tok, groups)
    here = BLOCK // per
    own = own_mask(per)
    for g in range(groups):
        for t in range(tok // here):
            lo = t * here
            prob = probs[g, t, lo:]
            prob = stack((jnp.where(own, 0.0, prob[:here]), 0, here), (prob, here, tok - lo))
            prob_grad = dot(back_value[g, lo:], grad[g, t * BLOCK : (t + 1) * BLOCK, :], NT)
            delta = own_delta[g, t] + jnp.sum(prob * prob_grad, axis=0, keepdims=True)
            delta_out[g, t] = delta
            back_score[g, t, lo:] = (prob * (prob_grad - delta)).astype(BF16)
    for g in range(groups):
        sums = [None] * (tok // here)
        for t in range(tok // here):
            rows = query[g, t * BLOCK : (t + 1) * BLOCK, :]
            add_rows(sums, t, dot(back_score[g, t, t * here :, :], rows), here)
        flat[pl.ds(g, tok, stride=groups), :] = jnp.concatenate(sums, axis=0)
    back[...] = flat[...].astype(BF16)


def query_kernel(sizes, probs, own_prob_grad, delta, back_score, query, own_key, back_key, unsort, query_grad, key_grad, part_grad, own_score):
    tok, heads, groups, per = sizes
    depth = own_key.shape[2]
    step = BLOCK // heads
    share = step * per
    here = BLOCK // per
    own = own_mask(per)
    for g in range(groups):
        for t in range(tok // here):
            lo, hi = t * here, (t + 1) * here
            out = probs[g, t, :hi] * (own_prob_grad[g, t, :hi] - delta[g, t])
            own_score[g, t, :hi] = stack((out, 0, lo), (jnp.where(own, out[lo:], 0.0), 0, here)).astype(BF16)
    for g in range(groups):
        for t in range(tok // here):
            lo, hi = t * here, (t + 1) * here
            keys = jnp.concatenate([own_key[g, :hi], back_key[g, lo:]], axis=0)
            both = jnp.concatenate([own_score[g, t, :hi], back_score[g, t, lo:]], axis=0)
            part_grad[g, t * BLOCK : (t + 1) * BLOCK, :] = dot(both, keys, TN)
    for g in range(groups):
        sums = [None] * (tok // here)
        for t in range(tok // here):
            rows = query[g, t * BLOCK : (t + 1) * BLOCK, :]
            add_rows(sums, 0, dot(own_score[g, t, : (t + 1) * here, :], rows), here)
        key_grad[pl.ds(g, tok, stride=groups), :] = jnp.concatenate(sums, axis=0)
    for b in range(0, tok // step, 2):
        both = [
            jnp.concatenate([part_grad[g, (b + i) * share : (b + i + 1) * share, :] for g in range(groups)], axis=0)
            for i in range(2)
        ]
        both = jnp.concatenate(both, axis=1)
        high = both.astype(BF16)
        low = (both - high.astype(F32)).astype(BF16)
        both = dot(unsort[...], high) + dot(unsort[...], low)
        query_grad[b * BLOCK : (b + 1) * BLOCK, :] = both[:, :depth]
        query_grad[(b + 1) * BLOCK : (b + 2) * BLOCK, :] = both[:, depth:]


def factor_of(count, tokens, depth):
    last = count.shape[1] - 1
    return (tokens / count[0:1, last : last + 1].astype(F32)) * (1.0 / math.sqrt(depth))


def query_out_kernel(tokens, count, query_in, query_out, factor_out, query_grad, sems):
    rows, depth = query_in.shape
    factor = factor_of(count, tokens, depth)
    factor_out[...] = jnp.broadcast_to(factor, factor_out.shape)
    copies = []
    for i in range(PIECES):
        part = pl.ds(i * (rows // PIECES), rows // PIECES)
        query_grad[part, :] = (query_in[part, :] * factor).astype(BF16)
        copies.append(pltpu.make_async_copy(query_grad.at[part], query_out.at[part], sems.at[i]))
        copies[-1].start()
    for copy in copies:
        copy.wait()


VMEM = pl.BlockSpec(memory_space=pltpu.VMEM)
HBM = pl.BlockSpec(memory_space=pltpu.HBM)


def call(kernel, ins, outs, scratch=(), flops=None, out_spec=VMEM):
    return pl.pallas_call(
        kernel,
        out_shape=[jax.ShapeDtypeStruct(shape, dtype) for shape, dtype in outs],
        in_specs=ins,
        out_specs=out_spec if isinstance(out_spec, list) else [out_spec] * len(outs),
        scratch_shapes=list(scratch),
        cost_estimate=None if flops is None else pl.CostEstimate(flops=flops, bytes_accessed=0, transcendentals=0),
        compiler_params=pltpu.CompilerParams(vmem_limit_bytes=32 * 1024 * 1024),
    )


def partner(value, axis, hop):
    return lax.ppermute(value, axis, [(i, i ^ hop) for i in range(lax.axis_size(axis))])


def add_partner(value, axis, hop):
    return value + partner(value, axis, hop)


def per_device(query_rows, key_rows, value_matrix, out_grad, offsets, query_head_group):
    _, tok, heads, depth = query_rows.shape
    groups = key_rows.shape[2]
    per = heads // groups
    sizes = (tok, heads, groups, per)
    ctx = lax.axis_size("ctx")
    tokens = float(offsets.shape[0] * lax.axis_size("dp") * tok * ctx)
    axes, copies = ("ctx", "dp"), lax.axis_size("dp")
    swap = 1 if copies % 2 == 0 else 0
    ahead = [(c * copies + i, (c + 1) * copies + i) for c in range(ctx - 1) for i in range(copies)]
    behind = [(b, a) for a, b in ahead] + [(i ^ swap, (ctx - 1) * copies + i) for i in range(copies)]
    keys_ahead = ahead + [((ctx - 1) * copies + i, i ^ swap) for i in range(copies)]
    ahead = ahead + [((ctx - 1) * copies + i, i) for i in range(copies)]

    back_key = lax.ppermute(key_rows, axes, keys_ahead).reshape(tok * groups, depth)
    back_value = lax.ppermute(value_matrix, axes, ahead).reshape(tok * groups, depth)
    dp = lax.axis_size("dp")
    paired = dp >= 8 and dp & (dp - 1) == 0
    hops = [1 << i for i in range(dp.bit_length() - 1)] if paired else []
    sorted_shape = (groups, tok * per, depth)
    packed = (tok * groups, depth)
    split = (groups, tok, depth)
    here = BLOCK // per
    (places,) = call(functools.partial(place_kernel, sizes), [], [((tok, tok * per), jnp.int32)], flops=1_000_000_000)()
    sort, unsort, bias = call(
        functools.partial(plan_kernel, sizes),
        [VMEM] * 3,
        [((BLOCK, BLOCK), BF16), ((BLOCK, BLOCK), BF16), ((tok, tok * per), F32)],
    )(offsets, query_head_group.reshape(1, heads), places)
    if paired:
        count, sort = lax.optimization_barrier((add_partner(offsets, "dp", 1), sort))
        moved = partner(count, "dp", hops[-1] | 1)
    else:
        moved = lax.psum(offsets, "dp")
    sorted_query, sorted_grad, own_key, own_value = call(
        functools.partial(arrange_kernel, sizes),
        [VMEM] * 5,
        [(sorted_shape, BF16), (sorted_shape, BF16), (split, BF16), (split, BF16)],
        [pltpu.VMEM(packed, F32)],
    )(
        sort,
        query_rows.reshape(tok * heads, depth),
        out_grad.reshape(tok * heads, depth),
        key_rows.reshape(packed),
        value_matrix.reshape(packed),
    )

    tall = (groups, tok // here, tok, BLOCK)
    line = (groups, tok // here, 1, BLOCK)
    probs, own_prob_grad, own_delta, back_key = call(
        functools.partial(probs_kernel, sizes),
        [VMEM] * 6,
        [(tall, F32), (tall, F32), (line, F32), (split, BF16)],
        [pltpu.VMEM(packed, F32)],
        500_000_000,
    )(bias, sorted_query, sorted_grad, own_key, own_value, back_key)
    moved, probs = lax.optimization_barrier((moved, probs))
    if paired:
        for hop in hops[2:-1]:
            count = count + moved
            moved = partner(count, "dp", hop)
    back_score, delta, back = call(
        functools.partial(score_kernel, sizes),
        [VMEM] * 5,
        [(tall, BF16), (line, F32), (packed, BF16)],
        [pltpu.VMEM(split, BF16), pltpu.VMEM(packed, F32)],
        2_000_000_000,
    )(probs, own_delta, sorted_query, sorted_grad, back_value)

    moved, back = lax.optimization_barrier((moved, back))
    back = lax.ppermute(back, axes, behind)
    if paired:
        count, delta = lax.optimization_barrier((count + moved, delta))
        count = add_partner(count, "dp", 2)
    else:
        count = moved

    plain_grad, own = call(
        functools.partial(query_kernel, sizes),
        [VMEM] * 8,
        [((tok * heads, depth), F32), (packed, F32)],
        [pltpu.VMEM(sorted_shape, F32), pltpu.VMEM(tall, BF16)],
    )(probs, own_prob_grad, delta, back_score, sorted_query, own_key, back_key, unsort)
    query_grad, factor = call(
        functools.partial(query_out_kernel, tokens),
        [VMEM] * 2,
        [((tok * heads, depth), BF16), ((1, depth), F32)],
        [pltpu.VMEM((tok * heads, depth), BF16), pltpu.SemaphoreType.DMA((PIECES,))],
        out_spec=[HBM, VMEM],
    )(count, plain_grad)
    key_grad = ((own + back.astype(F32)) * factor).astype(BF16)
    return (query_grad.reshape(query_rows.shape), key_grad.reshape(key_rows.shape))


def solution(mesh):
    return jax.shard_map(
        per_device,
        mesh=mesh,
        in_specs=(
            P("dp", "ctx", None, None),
            P("dp", "ctx", None, None),
            P("dp", "ctx", None, None),
            P("dp", "ctx", None, None),
            P("dp", None),
            P(),
        ),
        out_specs=(P("dp", "ctx", None, None), P("dp", "ctx", None, None)),
        check_vma=False,
    )
```

```python
import functools
import math

import jax
import jax.numpy as jnp
from jax import lax
from jax.experimental import pallas as pl
from jax.experimental.pallas import tpu as pltpu
from jax.sharding import PartitionSpec as P

NT = (((1,), (1,)), ((), ()))
NN = (((1,), (0,)), ((), ()))
TN = (((0,), (0,)), ((), ()))
F32, BF16 = jnp.float32, jnp.bfloat16
BLOCK = 256
PIECES = 4


def dot(a, b, dims=NN):
    return lax.dot_general(a, b, dims, preferred_element_type=F32)


def stack(*spans):
    pieces = [v[a:b] for v, a, b in spans if b > a]
    return pieces[0] if len(pieces) == 1 else jnp.concatenate(pieces, axis=0)


def split_heads(packed, flat, out, rows, groups):
    flat[...] = packed[...].astype(F32)
    for g in range(groups):
        out[g] = flat[pl.ds(g, rows, stride=groups), :].astype(BF16)


def place_kernel(sizes, places):
    tok, heads, groups, per = sizes
    shape = (tok, tok * per)
    col = lax.broadcasted_iota(jnp.int32, shape, 0)
    row = lax.broadcasted_iota(jnp.int32, shape, 1) // per
    places[...] = col - jnp.where(col > row, tok, 0)


def plan_kernel(sizes, bounds, group, places, sort, unsort, bias):
    tok, heads, groups, per = sizes
    step = BLOCK // heads
    share = step * per
    first = lax.broadcasted_iota(jnp.int32, (heads, heads), 0)
    second = lax.broadcasted_iota(jnp.int32, (heads, heads), 1)
    along = jnp.broadcast_to(group[...], (heads, heads))
    down = jnp.sum(jnp.where(first == second, along, 0), axis=1, keepdims=True)
    earlier = (first < second) & (down == along)
    slot = group[...] * share + jnp.sum(jnp.where(earlier, 1, 0), axis=0, keepdims=True)
    target = jnp.concatenate([slot + i * per for i in range(step)], axis=1)
    rows = lax.broadcasted_iota(jnp.int32, (BLOCK, BLOCK), 0)
    moves = jnp.where(rows == target, 1.0, 0.0).astype(F32)
    unsort[...] = moves.T.astype(BF16)
    sort[...] = moves.astype(BF16)
    start = lax.axis_index("ctx") * tok
    row = lax.broadcasted_iota(jnp.int32, (8, tok * per), 1) // per
    place = row + start
    low = jnp.zeros_like(place)
    last = bounds.shape[1] - 1
    for i in range(1, last):
        low = jnp.where(place >= bounds[:, i : i + 1], bounds[:, i : i + 1], low)
    low = jnp.where(place >= bounds[:, last : last + 1], jnp.int32(1 << 30), low) - start
    for c in range(0, tok, 8):
        bias[c : c + 8, :] = jnp.where(places[c : c + 8, :] >= low, 0.0, -1e30).astype(F32)


def arrange_kernel(sizes, sort, query, grad, key, value, sorted_query, sorted_grad, own_key, own_value, flat):
    tok, heads, groups, per = sizes
    step = BLOCK // heads
    share = step * per
    depth = query.shape[1]
    for b in range(tok // step):
        part = slice(b * BLOCK, (b + 1) * BLOCK)
        both = jnp.concatenate([query[part, :], grad[part, :]], axis=1)
        both = dot(sort[...], both).astype(BF16)
        for g in range(groups):
            sorted_query[g, b * share : (b + 1) * share, :] = both[g * share : (g + 1) * share, :depth]
            sorted_grad[g, b * share : (b + 1) * share, :] = both[g * share : (g + 1) * share, depth:]
    split_heads(key, flat, own_key, tok, groups)
    split_heads(value, flat, own_value, tok, groups)


def own_mask(per):
    here = BLOCK // per
    shape = (here, BLOCK)
    return lax.broadcasted_iota(jnp.int32, shape, 0) <= lax.broadcasted_iota(jnp.int32, shape, 1) // per


def merge(left, right, t, own):
    here = own.shape[0]
    lo, hi = t * here, (t + 1) * here
    mid = jnp.where(own, left[lo:hi], right[:here])
    return stack((left, 0, lo), (mid, 0, here), (right, here, right.shape[0]))


def probs_kernel(sizes, bias, query, grad, own_key, own_value, back_in, probs, own_probs, own_prob_grad, own_delta, back_key, flat):
    tok, heads, groups, per = sizes
    split_heads(back_in, flat, back_key, tok, groups)
    rate = math.log2(math.e) / math.sqrt(query.shape[2])
    own = own_mask(per)
    here = BLOCK // per
    for g in range(groups):
        for t in range(tok // here):
            part = slice(t * BLOCK, (t + 1) * BLOCK)
            lo, hi = t * here, (t + 1) * here
            both = dot(jnp.concatenate([own_key[g, :hi], back_key[g, lo:]], axis=0), query[g, part, :], NT)
            scores = merge(both[:hi], both[hi:], t, own) + bias[:, part]
            top = jnp.maximum(jnp.max(scores, axis=0, keepdims=True), -1e29)
            terms = jnp.exp2((scores - top) * rate)
            scale = 1.0 / jnp.maximum(jnp.sum(terms, axis=0, keepdims=True), 1.0)
            prob = terms * scale
            own_probs[g, t, :hi] = stack((prob, 0, lo), (jnp.where(own, prob[lo:hi], 0.0), 0, here))
            probs[g, t, lo:] = stack((jnp.where(own, 0.0, prob[lo:hi]), 0, here), (prob, hi, tok))
            prob_grad = dot(own_value[g, :hi], grad[g, part, :], NT)
            own_prob_grad[g, t, :hi] = prob_grad
            own_delta[g, t] = jnp.sum(own_probs[g, t, :hi] * prob_grad, axis=0, keepdims=True)


def add_rows(sums, first, piece, here):
    for i in range(piece.shape[0] // here):
        block = piece[i * here : (i + 1) * here]
        sums[first + i] = block if sums[first + i] is None else sums[first + i] + block


def score_kernel(sizes, probs, own_delta, query, grad, value_in, back_score, delta_out, back, back_value, flat):
    tok, heads, groups, per = sizes
    split_heads(value_in, flat, back_value, tok, groups)
    here = BLOCK // per
    own = own_mask(per)
    for g in range(groups):
        for t in range(tok // here):
            lo = t * here
            prob = probs[g, t, lo:]
            prob_grad = dot(back_value[g, lo:], grad[g, t * BLOCK : (t + 1) * BLOCK, :], NT)
            delta = own_delta[g, t] + jnp.sum(prob * prob_grad, axis=0, keepdims=True)
            delta_out[g, t] = delta
            back_score[g, t, lo:] = (prob * (prob_grad - delta)).astype(BF16)
    for g in range(groups):
        sums = [None] * (tok // here)
        for t in range(tok // here):
            rows = query[g, t * BLOCK : (t + 1) * BLOCK, :]
            add_rows(sums, t, dot(back_score[g, t, t * here :, :], rows), here)
        flat[pl.ds(g, tok, stride=groups), :] = jnp.concatenate(sums, axis=0)
    back[...] = flat[...].astype(BF16)


def query_kernel(sizes, probs, own_prob_grad, delta, back_score, query, own_key, back_key, unsort, query_grad, key_grad, part_grad, own_score):
    tok, heads, groups, per = sizes
    depth = own_key.shape[2]
    step = BLOCK // heads
    share = step * per
    here = BLOCK // per
    own = own_mask(per)
    for g in range(groups):
        for t in range(tok // here):
            lo, hi = t * here, (t + 1) * here
            out = probs[g, t, :hi] * (own_prob_grad[g, t, :hi] - delta[g, t])
            own_score[g, t, :hi] = out.astype(BF16)
    for g in range(groups):
        for t in range(tok // here):
            lo, hi = t * here, (t + 1) * here
            keys = jnp.concatenate([own_key[g, :hi], back_key[g, lo:]], axis=0)
            both = jnp.concatenate([own_score[g, t, :hi], back_score[g, t, lo:]], axis=0)
            part_grad[g, t * BLOCK : (t + 1) * BLOCK, :] = dot(both, keys, TN)
    for g in range(groups):
        sums = [None] * (tok // here)
        for t in range(tok // here):
            rows = query[g, t * BLOCK : (t + 1) * BLOCK, :]
            add_rows(sums, 0, dot(own_score[g, t, : (t + 1) * here, :], rows), here)
        key_grad[pl.ds(g, tok, stride=groups), :] = jnp.concatenate(sums, axis=0)
    for b in range(0, tok // step, 2):
        both = [
            jnp.concatenate([part_grad[g, (b + i) * share : (b + i + 1) * share, :] for g in range(groups)], axis=0)
            for i in range(2)
        ]
        both = jnp.concatenate(both, axis=1)
        high = both.astype(BF16)
        low = (both - high.astype(F32)).astype(BF16)
        both = dot(unsort[...], high) + dot(unsort[...], low)
        query_grad[b * BLOCK : (b + 1) * BLOCK, :] = both[:, :depth]
        query_grad[(b + 1) * BLOCK : (b + 2) * BLOCK, :] = both[:, depth:]


def factor_of(count, tokens, depth):
    last = count.shape[1] - 1
    return (tokens / count[0:1, last : last + 1].astype(F32)) * (1.0 / math.sqrt(depth))


def query_out_kernel(tokens, count, query_in, query_out, factor_out, query_grad, sems):
    rows, depth = query_in.shape
    factor = factor_of(count, tokens, depth)
    factor_out[...] = jnp.broadcast_to(factor, factor_out.shape)
    copies = []
    for i in range(PIECES):
        part = pl.ds(i * (rows // PIECES), rows // PIECES)
        query_grad[part, :] = (query_in[part, :] * factor).astype(BF16)
        copies.append(pltpu.make_async_copy(query_grad.at[part], query_out.at[part], sems.at[i]))
        copies[-1].start()
    for copy in copies:
        copy.wait()


VMEM = pl.BlockSpec(memory_space=pltpu.VMEM)
HBM = pl.BlockSpec(memory_space=pltpu.HBM)


def call(kernel, ins, outs, scratch=(), flops=None, out_spec=VMEM):
    return pl.pallas_call(
        kernel,
        out_shape=[jax.ShapeDtypeStruct(shape, dtype) for shape, dtype in outs],
        in_specs=ins,
        out_specs=out_spec if isinstance(out_spec, list) else [out_spec] * len(outs),
        scratch_shapes=list(scratch),
        cost_estimate=None if flops is None else pl.CostEstimate(flops=flops, bytes_accessed=0, transcendentals=0),
        compiler_params=pltpu.CompilerParams(vmem_limit_bytes=32 * 1024 * 1024),
    )


def partner(value, axis, hop):
    return lax.ppermute(value, axis, [(i, i ^ hop) for i in range(lax.axis_size(axis))])


def add_partner(value, axis, hop):
    return value + partner(value, axis, hop)


def per_device(query_rows, key_rows, value_matrix, out_grad, offsets, query_head_group):
    _, tok, heads, depth = query_rows.shape
    groups = key_rows.shape[2]
    per = heads // groups
    sizes = (tok, heads, groups, per)
    ctx = lax.axis_size("ctx")
    tokens = float(offsets.shape[0] * lax.axis_size("dp") * tok * ctx)
    axes, copies = ("ctx", "dp"), lax.axis_size("dp")
    swap = 1 if copies % 2 == 0 else 0
    ahead = [(c * copies + i, (c + 1) * copies + i) for c in range(ctx - 1) for i in range(copies)]
    behind = [(b, a) for a, b in ahead] + [(i ^ swap, (ctx - 1) * copies + i) for i in range(copies)]
    keys_ahead = ahead + [((ctx - 1) * copies + i, i ^ swap) for i in range(copies)]
    ahead = ahead + [((ctx - 1) * copies + i, i) for i in range(copies)]

    back_key = lax.ppermute(key_rows, axes, keys_ahead).reshape(tok * groups, depth)
    back_value = lax.ppermute(value_matrix, axes, ahead).reshape(tok * groups, depth)
    dp = lax.axis_size("dp")
    paired = dp >= 8 and dp & (dp - 1) == 0
    hops = [1 << i for i in range(dp.bit_length() - 1)] if paired else []
    sorted_shape = (groups, tok * per, depth)
    packed = (tok * groups, depth)
    split = (groups, tok, depth)
    here = BLOCK // per
    (places,) = call(functools.partial(place_kernel, sizes), [], [((tok, tok * per), jnp.int32)], flops=1_000_000_000)()
    sort, unsort, bias = call(
        functools.partial(plan_kernel, sizes),
        [VMEM] * 3,
        [((BLOCK, BLOCK), BF16), ((BLOCK, BLOCK), BF16), ((tok, tok * per), F32)],
    )(offsets, query_head_group.reshape(1, heads), places)
    if paired:
        count, sort = lax.optimization_barrier((add_partner(offsets, "dp", 1), sort))
        moved = partner(count, "dp", hops[-1])
    else:
        moved = lax.psum(offsets, "dp")
    sorted_query, sorted_grad, own_key, own_value = call(
        functools.partial(arrange_kernel, sizes),
        [VMEM] * 5,
        [(sorted_shape, BF16), (sorted_shape, BF16), (split, BF16), (split, BF16)],
        [pltpu.VMEM(packed, F32)],
    )(
        sort,
        query_rows.reshape(tok * heads, depth),
        out_grad.reshape(tok * heads, depth),
        key_rows.reshape(packed),
        value_matrix.reshape(packed),
    )

    tall = (groups, tok // here, tok, BLOCK)
    line = (groups, tok // here, 1, BLOCK)
    probs, own_probs, own_prob_grad, own_delta, back_key = call(
        functools.partial(probs_kernel, sizes),
        [VMEM] * 6,
        [(tall, F32), (tall, F32), (tall, F32), (line, F32), (split, BF16)],
        [pltpu.VMEM(packed, F32)],
        500_000_000,
    )(bias, sorted_query, sorted_grad, own_key, own_value, back_key)
    moved, probs = lax.optimization_barrier((moved, probs))
    if paired:
        for hop in hops[2:-1]:
            count = count + moved
            moved = partner(count, "dp", hop)
    back_score, delta, back = call(
        functools.partial(score_kernel, sizes),
        [VMEM] * 5,
        [(tall, BF16), (line, F32), (packed, BF16)],
        [pltpu.VMEM(split, BF16), pltpu.VMEM(packed, F32)],
        2_000_000_000,
    )(probs, own_delta, sorted_query, sorted_grad, back_value)

    moved, back = lax.optimization_barrier((moved, back))
    back = lax.ppermute(back, axes, behind)
    if paired:
        count, delta = lax.optimization_barrier((count + moved, delta))
        count = add_partner(count, "dp", 2)
    else:
        count = moved

    plain_grad, own = call(
        functools.partial(query_kernel, sizes),
        [VMEM] * 8,
        [((tok * heads, depth), F32), (packed, F32)],
        [pltpu.VMEM(sorted_shape, F32), pltpu.VMEM(tall, BF16)],
    )(own_probs, own_prob_grad, delta, back_score, sorted_query, own_key, back_key, unsort)
    query_grad, factor = call(
        functools.partial(query_out_kernel, tokens),
        [VMEM] * 2,
        [((tok * heads, depth), BF16), ((1, depth), F32)],
        [pltpu.VMEM((tok * heads, depth), BF16), pltpu.SemaphoreType.DMA((PIECES,))],
        out_spec=[HBM, VMEM],
    )(count, plain_grad)
    key_grad = ((own + back.astype(F32)) * factor).astype(BF16)
    return (query_grad.reshape(query_rows.shape), key_grad.reshape(key_rows.shape))


def solution(mesh):
    return jax.shard_map(
        per_device,
        mesh=mesh,
        in_specs=(
            P("dp", "ctx", None, None),
            P("dp", "ctx", None, None),
            P("dp", "ctx", None, None),
            P("dp", "ctx", None, None),
            P("dp", None),
            P(),
        ),
        out_specs=(P("dp", "ctx", None, None), P("dp", "ctx", None, None)),
        check_vma=False,
    )
```
